32 devices in a mesh: ifg: 4 (over x, core), rows: 8 (over z, y).
Axes of the slice: x: 2, y: 2, z: 4, core: 2. Of those that a mesh axis runs over, the one named last changes fastest.
Arguments:
- phase: bfloat16 [512, 64, 512], P('ifg', 'rows')
- coherence: bfloat16 [512, 64, 512], P('ifg', 'rows'), may hold values from 0.0996 to 0.95
- height: float32 [64, 512], P('rows')
- gap_mask: int32 [512, 64], P('ifg', 'rows'), may hold values 0 or 1
- date_pairs: int32 [512, 2], replicated, may hold values from 0 to 299, as said below
Outputs:
- displacement: float32 [300, 64, 512], P(None, 'rows', 'ifg')
- topo_slope: float32 [512], P('ifg')
The draws below stay inside these ranges and needn't reach their ends.
Inputs may be any that keep to these rules, and one draw needn't show every extreme that they name: date_pairs[i, 0] < date_pairs[i, 1] for every interferogram.
All inputs are finite; a program needn't handle non-finite values. No bound on the sum of `gap_mask` on one device may be relied on, other than what follows from the above.
Results may differ from the reference program's by a relative error of at most 0.0028.
Values may be sent and summed in bfloat16 or wider, within the bound.
A program may use at most 128 MiB of HBM per device.

```python
import jax
import jax.numpy as jnp
from jax import lax

IFGS = 512
DATES = 300
R_DEV = 8
C_DEV = 128
ITERS = 3
IMG_ROWS = 64
COLS = 512
N_ROWS = 8


def height_field(key):
    height_key = jax.random.fold_in(key, 11)
    row_ramp = 1.0 + 2.0 * jnp.arange(IMG_ROWS, dtype=jnp.float32) / IMG_ROWS
    rough = jnp.clip(jax.random.normal(height_key, (IMG_ROWS, COLS), jnp.float32), -6.0, 6.0)
    return jnp.clip(row_ramp[:, None] * rough, -18.0, 18.0)


def draw_height(key, part):
    return height_field(key)


def draw_phase(key, part):
    terrain = height_field(key)
    slopes = jax.random.uniform(jax.random.fold_in(key, 23), (IFGS,), jnp.float32, -0.5, 0.5)
    noise_key = jax.random.fold_in(key, 31)
    noise_field = jnp.clip(jax.random.normal(noise_key, (IFGS, IMG_ROWS, COLS), jnp.float32), -6.0, 6.0)
    return (noise_field + slopes[:, None, None] * terrain[None]).astype(jnp.bfloat16)


def draw_coherence(key, part):
    base_key = jax.random.fold_in(key, 51)
    shape = (IFGS, IMG_ROWS, COLS)
    base = jax.random.uniform(base_key, shape, jnp.float32)
    col_blocks = COLS // C_DEV
    order = jax.random.permutation(jax.random.fold_in(key, 53), col_blocks).astype(jnp.float32)
    col_level = -1.5 + 3.0 * order / (col_blocks - 1)
    row_level = jax.random.uniform(jax.random.fold_in(key, 57), (IMG_ROWS // R_DEV,), jnp.float32, -0.75, 0.75)
    exponent = jnp.exp(jnp.repeat(row_level, R_DEV)[:, None] + jnp.repeat(col_level, C_DEV)[None, :])
    return (0.1 + 0.85 * jnp.power(base, exponent[None])).astype(jnp.bfloat16)


def draw_date_pairs(key, part):
    earlier = jax.random.randint(jax.random.fold_in(key, 41), (IFGS,), 0, DATES - 1)
    date_gap = jax.random.randint(jax.random.fold_in(key, 43), (IFGS,), 1, 13)
    earlier = earlier.at[0].set(0)
    later = jnp.minimum(earlier + date_gap, DATES - 1)
    later = later.at[IFGS - 1].set(DATES - 1)
    return jnp.stack([earlier, later], axis=1).astype(jnp.int32)


def plant(array, stream_key, low, top_value):
    place = [jax.random.randint(jax.random.fold_in(stream_key, axis), (), 0, length) for axis, length in enumerate(array.shape)]
    longest = array.shape.index(max(array.shape))
    beside = place[:longest] + [(place[longest] + 1) % array.shape[longest]] + place[longest + 1:]
    return array.at[tuple(place)].set(low).at[tuple(beside)].set(top_value)


def setup_inputs(seed: int = 0) -> dict:
    key_list = jax.random.split(jax.random.key(seed), 6)
    phase = draw_phase(jax.random.fold_in(key_list[5], 71), 0)
    coherence = draw_coherence(jax.random.fold_in(key_list[5], 71), 0)
    height = draw_height(jax.random.fold_in(key_list[5], 71), 0)
    gap_mask = plant((jax.random.randint(key_list[3], (IFGS, IMG_ROWS), 0, 8) < 7).astype(jnp.int32), jax.random.fold_in(key_list[3], 1), 0, 1)
    date_pairs = draw_date_pairs(jax.random.fold_in(key_list[5], 71), 0)
    return {"phase": phase, "coherence": coherence, "height": height, "gap_mask": gap_mask, "date_pairs": date_pairs}


SMOOTHING_WEIGHT = 0.5
RIDGE_WEIGHT = 0.05


def box_sum(values):
    padded = jnp.pad(values, 1)
    row_sum = padded[:-2] + padded[1:-1] + padded[2:]
    return row_sum[:, :-2] + row_sum[:, 1:-1] + row_sum[:, 2:]


def reference(phase, coherence, height, gap_mask, date_pairs):
    def per_interferogram(entries):
        phase_one, coher_one, mask_one = entries
        coher_f = coher_one.astype(jnp.float32)
        top_sum = box_sum(coher_f * phase_one.astype(jnp.float32))
        low_sum = box_sum(coher_f)
        smooth = top_sum / low_sum
        mean_coh = low_sum / 9.0
        topo = jnp.sum(mean_coh * smooth * height) / jnp.sum(mean_coh * height * height)
        corrected = (smooth - topo * height).astype(jnp.bfloat16)
        weights = (mask_one.astype(jnp.float32)[:, None] * mean_coh).astype(jnp.bfloat16)
        return corrected, weights, topo

    corrected, weights, topo_slope = lax.map(per_interferogram, (phase, coherence, gap_mask))
    earlier = date_pairs[:, 0]
    later = date_pairs[:, 1]

    def slab_term(values, use_field):
        def one_slab(slab_index):
            start = (slab_index * R_DEV).astype(jnp.int32)
            weight_slab = lax.dynamic_slice_in_dim(weights, start, R_DEV, 1).astype(jnp.float32)
            if use_field:
                value_slab = lax.dynamic_slice_in_dim(values, start, R_DEV, 1)
                diffs = jnp.take(value_slab, later, axis=0) - jnp.take(value_slab, earlier, axis=0)
            else:
                diffs = lax.dynamic_slice_in_dim(corrected, start, R_DEV, 1).astype(jnp.float32)
            scaled = diffs * weight_slab
            return (jax.ops.segment_sum(scaled, later, DATES) - jax.ops.segment_sum(scaled, earlier, DATES))

        stacked = lax.map(one_slab, jnp.arange(N_ROWS, dtype=jnp.int32))
        return stacked.transpose(1, 0, 2, 3).reshape(DATES, IMG_ROWS, COLS)

    def operate(values):
        padded = jnp.pad(values, ((0, 0), (1, 1), (1, 1)))
        neighbours = padded[:, 2:, 1:-1] + padded[:, :-2, 1:-1] + padded[:, 1:-1, 2:] + padded[:, 1:-1, :-2]
        spread = 4.0 * values - neighbours
        return slab_term(values, True) + SMOOTHING_WEIGHT * spread + RIDGE_WEIGHT * values

    right_side = slab_term(None, False)
    displacement = jnp.zeros_like(right_side)
    residual, direction = right_side, right_side
    norm_now = jnp.sum(residual * residual)
    for sweep_index in range(ITERS):
        mapped = operate(direction)
        step_size = norm_now / jnp.sum(direction * mapped)
        displacement = displacement + step_size * direction
        residual = residual - step_size * mapped
        norm_next = jnp.sum(residual * residual)
        direction = residual + (norm_next / norm_now) * direction
        norm_now = norm_next
    return displacement, topo_slope
```

```python
import functools

import jax
import jax.numpy as jnp
from jax import lax
from jax.experimental import pallas as pl
from jax.experimental.pallas import tpu as pltpu
from jax.sharding import PartitionSpec as P

DATES = 300
DPAD = 304
KPAD = 384
LANES = 128
CHUNK = 16
SMOOTHING_WEIGHT = 0.5
RIDGE_WEIGHT = 0.05
F32 = jnp.float32
BF16 = jnp.bfloat16
MESH = pl.DeviceIdType.MESH


def split(value):
    high = value.astype(BF16)
    low = (value - high.astype(F32)).astype(BF16)
    return high, low


def dot(a, b):
    return jnp.dot(a, b, preferred_element_type=F32)


def kernel(
    n, m,
    phase, coher, height, gap, pairs,
    out, topo_out,
    ph_s, co_s, edge, halo, sm_s, w_send, w_all, c_send, c_all,
    mom, mom_all, topo_s, g, gt, vb,
    r_s, w_s, n_s, p_s, s_s, z_s,
    pack, halo_row, halo_col, red_a, red_b,
    halo_sems, w_sems, c_sems, own_sems, mom_sems, row_sems, col_sems, a_sems, b_sems,
):
    count, rows, width = phase.shape
    ifgs = pairs.shape[1]
    tiles = width // LANES
    chunks = count // CHUNK
    me = lax.axis_index("ifg")
    my_row = lax.axis_index("rows")
    has_up, has_down = my_row > 0, my_row < m - 1
    has_left, has_right = me > 0, me < n - 1

    barrier = pltpu.get_barrier_semaphore()
    for k in range(1, n):
        pl.semaphore_signal(barrier, inc=1, device_id=(lax.rem(me + k, n), my_row), device_id_type=MESH)
    for k in range(1, m):
        pl.semaphore_signal(barrier, inc=1, device_id=(me, lax.rem(my_row + k, m)), device_id_type=MESH)

    def remote(src, dst, sems, index, target):
        return pltpu.make_async_remote_copy(
            src_ref=src, dst_ref=dst,
            send_sem=sems.at[(0,) + index], recv_sem=sems.at[(1,) + index],
            device_id=target, device_id_type=MESH,
        )

    def widen(c, _):
        for src, dst in ((phase, ph_s), (coher, co_s)):
            block = src[pl.ds(c * CHUNK, CHUNK)].astype(F32).reshape(CHUNK * rows, width)
            for t in range(tiles):
                dst[t, pl.ds(pl.multiple_of(c * CHUNK * rows, CHUNK * rows), CHUNK * rows), :] = (
                    block[:, t * LANES:(t + 1) * LANES]
                )
        return 0

    lax.fori_loop(0, chunks, widen, 0)

    def row_of(ref, j, i0, size):
        return jnp.concatenate(
            [ref[t, pl.ds(i0 * rows + j, size, stride=rows), :] for t in range(tiles)], axis=1
        )

    def take_edges(c, _):
        i0 = pl.multiple_of(c * CHUNK, CHUNK)
        for side, j in ((0, 0), (1, rows - 1)):
            for a, ref in ((0, ph_s), (1, co_s)):
                edge[side, a, pl.ds(i0, CHUNK), :] = row_of(ref, j, i0, CHUNK).astype(BF16)
        return 0

    lax.fori_loop(0, chunks, take_edges, 0)

    pl.semaphore_wait(barrier, n + m - 2)

    send_up = remote(edge.at[0], halo.at[1], halo_sems, (0,), (me, lax.max(my_row - 1, 0)))
    send_down = remote(edge.at[1], halo.at[0], halo_sems, (1,), (me, lax.min(my_row + 1, m - 1)))

    @pl.when(has_up)
    def _():
        send_up.start()

    @pl.when(has_down)
    def _():
        send_down.start()

    mom[...] = jnp.zeros_like(mom)
    lane = lax.broadcasted_iota(jnp.int32, (CHUNK, width), 1)

    def box(vert):
        before = jnp.where(lane == 0, 0.0, pltpu.roll(vert, 1, 1))
        after = jnp.where(lane == width - 1, 0.0, pltpu.roll(vert, width - 1, 1))
        return vert + before + after

    def smooth_rows(low, high):
        def body(c, _):
            i0 = pl.multiple_of(c * CHUNK, CHUNK)
            gaps = gap[pl.ds(i0, CHUNK), :].astype(F32)

            def load(j):
                if j < 0 or j == rows:
                    side = 0 if j < 0 else 1
                    ph = halo[side, 0, pl.ds(i0, CHUNK), :].astype(F32)
                    co = halo[side, 1, pl.ds(i0, CHUNK), :].astype(F32)
                else:
                    ph = row_of(ph_s, j, i0, CHUNK)
                    co = row_of(co_s, j, i0, CHUNK)
                return ph * co, co

            window = [load(low - 1), load(low)]
            top_sum = jnp.zeros((CHUNK, LANES), F32)
            low_sum = jnp.zeros((CHUNK, LANES), F32)
            for j in range(low, high):
                window.append(load(j + 1))
                numer = box(window[0][0] + window[1][0] + window[2][0])
                denom = box(window[0][1] + window[1][1] + window[2][1])
                window.pop(0)
                smooth = numer / denom
                mean = denom * (1.0 / 9.0)
                weight = (gaps[:, j:j + 1] * mean).astype(BF16)
                for d in range(n):
                    w_send[d, j, pl.ds(i0, CHUNK), :] = weight[:, d * LANES:(d + 1) * LANES]
                sm_s[j, pl.ds(i0, CHUNK), :] = smooth
                terrain = height[j:j + 1, :]
                scaled = mean * terrain
                top = scaled * smooth
                low_part = scaled * terrain
                for t in range(tiles):
                    top_sum += top[:, t * LANES:(t + 1) * LANES]
                    low_sum += low_part[:, t * LANES:(t + 1) * LANES]
            mom[0, pl.ds(i0, CHUNK), :] += top_sum
            mom[1, pl.ds(i0, CHUNK), :] += low_sum
            return 0

        lax.fori_loop(0, chunks, body, 0)

    mine = pl.ds(pl.multiple_of(me * count, count), count)

    def exchange(src, dst, sems, part, low, high):
        span = pl.ds(low, high - low)
        copies = []
        for k in range(n - 1, 0, -1):
            d = lax.rem(me + k, n)
            copy = remote(src.at[d, span], dst.at[span, mine, :], sems, (part, k), (d, my_row))
            copy.start()
            copies.append(copy)
        own = pltpu.make_async_copy(src.at[me, span], dst.at[span, mine, :], sems.at[0, part, 0])
        own.start()
        copies.append(own)
        return copies

    half = rows // 2
    pending = []
    smooth_rows(1, half)
    pending += exchange(w_send, w_all, w_sems, 0, 1, half)
    smooth_rows(half, rows - 1)
    pending += exchange(w_send, w_all, w_sems, 1, half, rows - 1)

    date = lax.broadcasted_iota(jnp.int32, (KPAD, ifgs), 0)
    signs = (date == pairs[1:2, :]).astype(F32) - (date == pairs[0:1, :]).astype(F32)
    gt[...] = signs[:DPAD].astype(BF16)
    g[...] = signs.T.astype(BF16)
    vb[...] = jnp.zeros_like(vb)

    @pl.when(has_up)
    def _():
        send_up.wait_send()
        send_down.wait_recv()

    @pl.when(jnp.logical_not(has_up))
    def _():
        halo[0] = jnp.zeros_like(halo[0])

    @pl.when(has_down)
    def _():
        send_down.wait_send()
        send_up.wait_recv()

    @pl.when(jnp.logical_not(has_down))
    def _():
        halo[1] = jnp.zeros_like(halo[1])

    smooth_rows(0, 1)
    smooth_rows(rows - 1, rows)

    top_row = jnp.sum(mom[0].T, axis=0, keepdims=True)
    low_row = jnp.sum(mom[1].T, axis=0, keepdims=True)
    mom_all[my_row] = jnp.concatenate([top_row, low_row, jnp.zeros((6, LANES), F32)], axis=0)
    mom_copies = []
    for k in range(1, m):
        copy = remote(mom_all.at[my_row], mom_all.at[my_row], mom_sems, (k,), (me, lax.rem(my_row + k, m)))
        copy.start()
        mom_copies.append(copy)
    pending += exchange(w_send, w_all, w_sems, 2, 0, 1)
    pending += exchange(w_send, w_all, w_sems, 3, rows - 1, rows)
    for copy in mom_copies:
        copy.wait()
    sums = mom_all[0]
    for k in range(1, m):
        sums = sums + mom_all[k]
    slope = sums[0:1, :] / sums[1:2, :]
    topo_out[...] = slope[:, :count]
    topo_s[...] = jnp.broadcast_to(slope, (LANES, LANES)).T

    def correct_rows(low, high):
        def body(c, _):
            i0 = pl.multiple_of(c * CHUNK, CHUNK)
            column = topo_s[pl.ds(i0, CHUNK), :]
            for j in range(low, high):
                for d in range(n):
                    cols = pl.ds(d * LANES, LANES)
                    value = sm_s[j, pl.ds(i0, CHUNK), cols] - column * height[j:j + 1, cols]
                    c_send[d, j, pl.ds(i0, CHUNK), :] = value.astype(BF16)
            return 0

        lax.fori_loop(0, chunks, body, 0)

    correct_rows(0, half)
    first = exchange(c_send, c_all, c_sems, 0, 0, half)
    correct_rows(half, rows)
    second = exchange(c_send, c_all, c_sems, 1, half, rows)

    def back_project(u):
        high, low = split(u)
        return dot(gt[...], high) + dot(gt[...], low)

    def right_rows(q, _):
        u = jnp.concatenate(
            [w_all[2 * q + i].astype(F32) * c_all[2 * q + i].astype(F32) for i in range(2)], axis=1
        )
        b = back_project(u)
        for i in range(2):
            r_s[2 * q + i] = b[:, i * LANES:(i + 1) * LANES]
        return 0

    for copy in pending:
        copy.wait()
    for copy in first:
        copy.wait()
    lax.fori_loop(0, half // 2, right_rows, 0)
    for copy in second:
        copy.wait()
    lax.fori_loop(half // 2, half, right_rows, 0)

    small = lax.broadcasted_iota(jnp.int32, (DPAD, LANES), 1)

    def start_halo(v, step):
        first_packed = jnp.zeros((DPAD, LANES), F32)
        last_packed = jnp.zeros((DPAD, LANES), F32)
        for j in range(rows):
            tile = v[j]
            first_packed = jnp.where(small == j, pltpu.roll(tile, j, 1) if j else tile, first_packed)
            last_packed = jnp.where(small == j, pltpu.roll(tile, j + 1, 1), last_packed)
        pack[step, 0] = first_packed
        pack[step, 1] = last_packed
        copies = (
            (has_up, remote(v.at[0], halo_row.at[step, 1], row_sems, (step, 0), (me, lax.max(my_row - 1, 0)))),
            (has_down, remote(v.at[rows - 1], halo_row.at[step, 0], row_sems, (step, 1), (me, lax.min(my_row + 1, m - 1)))),
            (has_left, remote(pack.at[step, 0], halo_col.at[step, 1], col_sems, (step, 0), (lax.max(me - 1, 0), my_row))),
            (has_right, remote(pack.at[step, 1], halo_col.at[step, 0], col_sems, (step, 1), (lax.min(me + 1, n - 1), my_row))),
        )
        for there, copy in copies:
            pl.when(there)(copy.start)
        return copies

    def wait_halo(copies, step):
        for there, copy in copies:
            pl.when(there)(copy.wait_send)
        for index, buffer in ((0, halo_row), (1, halo_col)):
            low_there, low_copy = copies[2 * index]
            high_there, high_copy = copies[2 * index + 1]
            for side, there, copy in ((0, low_there, high_copy), (1, high_there, low_copy)):
                pl.when(there)(copy.wait_recv)

                @pl.when(jnp.logical_not(there))
                def _(side=side, buffer=buffer):
                    buffer[step, side] = jnp.zeros((DPAD, LANES), F32)

    def apply(v, target, step, middle):
        copies = start_halo(v, step)

        def body(q, _):
            high, low = split(jnp.concatenate([v[2 * q], v[2 * q + 1]], axis=1))
            vb[0, :DPAD, :] = high
            vb[1, :DPAD, :] = low
            diff = dot(g[...], vb[0]) + dot(g[...], vb[1])
            u = jnp.concatenate(
                [diff[:, i * LANES:(i + 1) * LANES] * w_all[2 * q + i].astype(F32) for i in range(2)], axis=1
            )
            image = back_project(u)
            for i in range(2):
                target[2 * q + i] = image[:, i * LANES:(i + 1) * LANES]
            return 0

        lax.fori_loop(0, half // 2, body, 0)
        middle()
        lax.fori_loop(half // 2, half, body, 0)
        wait_halo(copies, step)
        left_col, right_col = halo_col[step, 0], halo_col[step, 1]
        for j in range(rows):
            here = v[j]
            above = v[j - 1] if j else halo_row[step, 0]
            below = v[j + 1] if j < rows - 1 else halo_row[step, 1]
            left_edge = pltpu.roll(left_col, LANES - j, 1) if j else left_col
            right_edge = pltpu.roll(right_col, LANES - 1 - j, 1)
            left = jnp.where(small == 0, left_edge, pltpu.roll(here, 1, 1))
            right = jnp.where(small == LANES - 1, right_edge, pltpu.roll(here, LANES - 1, 1))
            spread = 4.0 * here - (above + below + left + right)
            target[j] = target[j] + SMOOTHING_WEIGHT * spread + RIDGE_WEIGHT * here

    def fold(value):
        return jnp.sum(value, axis=0, keepdims=True)

    def reduce_first(step, parts):
        filled = list(parts) + [jnp.zeros((8 - len(parts), LANES), F32)]
        red_a[step, me] = jnp.concatenate(filled, axis=0)
        copies = []
        for k in range(1, n):
            copy = remote(red_a.at[step, me], red_a.at[step, me], a_sems, (step, k), (lax.rem(me + k, n), my_row))
            copy.start()
            copies.append(copy)
        return copies

    def reduce_second(step, copies):
        for copy in copies:
            copy.wait()
        total = red_a[step, 0]
        for k in range(1, n):
            total = total + red_a[step, k]
        red_b[step, my_row] = total
        later = []
        for k in range(1, m):
            copy = remote(red_b.at[step, my_row], red_b.at[step, my_row], b_sems, (step, k), (me, lax.rem(my_row + k, m)))
            copy.start()
            later.append(copy)
        return later

    def reduce_last(step, copies):
        for copy in copies:
            copy.wait()
        total = red_b[step, 0]
        for k in range(1, m):
            total = total + red_b[step, k]
        total = jnp.sum(total, axis=1, keepdims=True)
        return [total[i:i + 1, :] for i in range(3)]

    def overlapped(step, parts, v, target, apply_step):
        state = {"copies": reduce_first(step, parts)}

        def middle():
            state["copies"] = reduce_second(step, state["copies"])

        apply(v, target, apply_step, middle)
        return reduce_last(step, state["copies"])

    apply(r_s, w_s, 0, lambda: None)
    gamma_sum = jnp.zeros((1, LANES), F32)
    delta_sum = jnp.zeros((1, LANES), F32)
    for j in range(rows):
        gamma_sum += fold(r_s[j] * r_s[j])
        delta_sum += fold(r_s[j] * w_s[j])
    gamma, curve, _ = overlapped(0, (gamma_sum, delta_sum), w_s, n_s, 1)

    alpha = gamma / curve
    alpha_first = alpha
    gamma_sum = jnp.zeros((1, LANES), F32)
    delta_sum = jnp.zeros((1, LANES), F32)
    cross_sum = jnp.zeros((1, LANES), F32)
    for j in range(rows):
        p, s, z = r_s[j], w_s[j], n_s[j]
        r = p - alpha * s
        w = s - alpha * z
        p_s[j], s_s[j], z_s[j] = p, s, z
        r_s[j], w_s[j] = r, w
        gamma_sum += fold(r * r)
        delta_sum += fold(r * w)
        cross_sum += fold(r * s)
    gamma_next, delta, cross = overlapped(1, (gamma_sum, delta_sum, cross_sum), w_s, n_s, 2)

    beta = gamma_next / gamma
    gamma = gamma_next
    curve = delta + 2.0 * beta * cross + beta * beta * curve
    alpha = gamma / curve
    gamma_sum = jnp.zeros((1, LANES), F32)
    delta_sum = jnp.zeros((1, LANES), F32)
    cross_sum = jnp.zeros((1, LANES), F32)
    for j in range(rows):
        r, w = r_s[j], w_s[j]
        first_p = p_s[j]
        p = r + beta * first_p
        s = w + beta * s_s[j]
        z = n_s[j] + beta * z_s[j]
        r = r - alpha * s
        w = w - alpha * z
        p_s[j] = p
        r_s[j] = r
        z_s[j] = alpha_first * first_p + alpha * p
        gamma_sum += fold(r * r)
        delta_sum += fold(r * w)
        cross_sum += fold(r * s)
    copies = reduce_first(2, (gamma_sum, delta_sum, cross_sum))
    gamma_next, delta, cross = reduce_last(2, reduce_second(2, copies))
    beta = gamma_next / gamma
    curve = delta + 2.0 * beta * cross + beta * beta * curve
    alpha = gamma_next / curve
    for j in range(rows):
        x = z_s[j] + alpha * (r_s[j] + beta * p_s[j])
        out[pl.ds(j, DATES, stride=rows), :] = x[:DATES]


def solution(mesh):
    n, m = mesh.shape["ifg"], mesh.shape["rows"]

    def per_device(phase, coherence, height, gap_mask, date_pairs):
        count, rows, width = phase.shape
        ifgs = date_pairs.shape[0]
        tiles = width // LANES
        dma = pltpu.SemaphoreType.DMA
        state = pltpu.VMEM((rows, DPAD, LANES), F32)
        vmem = pl.BlockSpec(memory_space=pltpu.VMEM)
        displacement, topo = pl.pallas_call(
            functools.partial(kernel, n, m),
            out_shape=(
                jax.ShapeDtypeStruct((DATES * rows, LANES), F32),
                jax.ShapeDtypeStruct((1, count), F32),
            ),
            in_specs=[vmem] * 5,
            out_specs=(vmem, vmem),
            scratch_shapes=[
                pltpu.VMEM((tiles, count * rows, LANES), F32),
                pltpu.VMEM((tiles, count * rows, LANES), F32),
                pltpu.VMEM((2, 2, count, width), BF16),
                pltpu.VMEM((2, 2, count, width), BF16),
                pltpu.VMEM((rows, count, width), F32),
                pltpu.VMEM((n, rows, count, LANES), BF16),
                pltpu.VMEM((rows, ifgs, LANES), BF16),
                pltpu.VMEM((n, rows, count, LANES), BF16),
                pltpu.VMEM((rows, ifgs, LANES), BF16),
                pltpu.VMEM((2, LANES, LANES), F32),
                pltpu.VMEM((m, 8, LANES), F32),
                pltpu.VMEM((LANES, LANES), F32),
                pltpu.VMEM((ifgs, KPAD), BF16),
                pltpu.VMEM((DPAD, ifgs), BF16),
                pltpu.VMEM((2, KPAD, 2 * LANES), BF16),
                state, state, state, state, state, state,
                pltpu.VMEM((3, 2, DPAD, LANES), F32),
                pltpu.VMEM((3, 2, DPAD, LANES), F32),
                pltpu.VMEM((3, 2, DPAD, LANES), F32),
                pltpu.VMEM((3, n, 8, LANES), F32),
                pltpu.VMEM((3, m, 8, LANES), F32),
                dma((2, 2)),
                dma((2, 4, n)),
                dma((2, 2, n)),
                dma((1,)),
                dma((2, m)),
                dma((2, 3, 2)),
                dma((2, 3, 2)),
                dma((2, 3, n)),
                dma((2, 3, m)),
            ],
            compiler_params=pltpu.CompilerParams(
                collective_id=0, has_side_effects=True, vmem_limit_bytes=56 * 1024 * 1024
            ),
        )(phase, coherence, height, gap_mask, date_pairs.T)
        return displacement.reshape(DATES, rows, LANES), topo.reshape(count)

    return jax.shard_map(
        per_device,
        mesh=mesh,
        in_specs=(
            P("ifg", "rows", None),
            P("ifg", "rows", None),
            P("rows", None),
            P("ifg", "rows"),
            P(),
        ),
        out_specs=(P(None, "rows", "ifg"), P("ifg")),
        check_vma=False,
    )
```

```python
import functools

import jax
import jax.numpy as jnp
from jax import lax
from jax.experimental import pallas as pl
from jax.experimental.pallas import tpu as pltpu
from jax.sharding import PartitionSpec as P

DATES = 300
DPAD = 304
KPAD = 384
LANES = 128
CHUNK = 16
SMOOTHING_WEIGHT = 0.5
RIDGE_WEIGHT = 0.05
F32 = jnp.float32
BF16 = jnp.bfloat16
MESH = pl.DeviceIdType.MESH


def split(value):
    high = value.astype(BF16)
    low = (value - high.astype(F32)).astype(BF16)
    return high, low


def dot(a, b):
    return jnp.dot(a, b, preferred_element_type=F32)


def kernel(
    n, m,
    phase, coher, height, gap, pairs,
    out, topo_out,
    ph_s, co_s, edge, halo, sm_s, w_send, w_all, c_send, c_all,
    h_halo, gap_s, mom, mom_all, topo_s, g, gt, vb,
    r_s, w_s, n_s, p_s, s_s, z_s,
    pack, halo_row, halo_col, red_a, red_b,
    h_sems, halo_sems, w_sems, c_sems, mom_sems, row_sems, col_sems, a_sems, b_sems,
):
    count, rows, width = phase.shape
    ifgs = pairs.shape[1]
    tiles = width // LANES
    chunks = count // CHUNK
    me = lax.axis_index("ifg")
    my_row = lax.axis_index("rows")
    has_up, has_down = my_row > 0, my_row < m - 1
    has_left, has_right = me > 0, me < n - 1

    barrier = pltpu.get_barrier_semaphore()
    for k in range(1, n):
        pl.semaphore_signal(barrier, inc=1, device_id=(lax.rem(me + k, n), my_row), device_id_type=MESH)
    for k in range(1, m):
        pl.semaphore_signal(barrier, inc=1, device_id=(me, lax.rem(my_row + k, m)), device_id_type=MESH)

    def remote(src, dst, sems, index, target):
        return pltpu.make_async_remote_copy(
            src_ref=src, dst_ref=dst,
            send_sem=sems.at[(0,) + index], recv_sem=sems.at[(1,) + index],
            device_id=target, device_id_type=MESH,
        )

    def widen(c, _):
        for src, dst in ((phase, ph_s), (coher, co_s)):
            block = src[pl.ds(c * CHUNK, CHUNK)].astype(F32).reshape(CHUNK * rows, width)
            for t in range(tiles):
                dst[t, pl.ds(pl.multiple_of(c * CHUNK * rows, CHUNK * rows), CHUNK * rows), :] = (
                    block[:, t * LANES:(t + 1) * LANES]
                )
        return 0

    lax.fori_loop(0, chunks, widen, 0)

    def row_of(ref, j, i0, size):
        return jnp.concatenate(
            [ref[t, pl.ds(i0 * rows + j, size, stride=rows), :] for t in range(tiles)], axis=1
        )

    gap_s[...] = gap[...].astype(F32).T
    pl.semaphore_wait(barrier, n + m - 2)
    up, down = (me, lax.max(my_row - 1, 0)), (me, lax.min(my_row + 1, m - 1))

    def start_pair(sent_up, sent_down, landing, sems):
        to_up = remote(sent_up, landing.at[1], sems, (0,), up)
        to_down = remote(sent_down, landing.at[0], sems, (1,), down)
        pl.when(has_up)(to_up.start)
        pl.when(has_down)(to_down.start)
        return to_up, to_down

    def wait_pair(copies, landing):
        to_up, to_down = copies
        for there, sent, received, side in ((has_up, to_up, to_down, 0), (has_down, to_down, to_up, 1)):
            pl.when(there)(sent.wait_send)
            pl.when(there)(received.wait_recv)

            @pl.when(jnp.logical_not(there))
            def _(side=side):
                landing[side] = jnp.zeros_like(landing[side])

    terrain_copies = start_pair(height, height, h_halo, h_sems)

    def take_edges(c, _):
        i0 = pl.multiple_of(c * CHUNK, CHUNK)
        for side, j in ((0, 0), (1, rows - 1)):
            for a, ref in ((0, ph_s), (1, co_s)):
                edge[side, a, pl.ds(i0, CHUNK), :] = row_of(ref, j, i0, CHUNK).astype(BF16)
        return 0


    def box(vert):
        lane = lax.broadcasted_iota(jnp.int32, vert.shape, 1)
        before = jnp.where(lane == 0, 0.0, pltpu.roll(vert, 1, 1))
        after = jnp.where(lane == width - 1, 0.0, pltpu.roll(vert, width - 1, 1))
        return vert + before + after

    def smooth_rows(low, high):
        def body(c, _):
            i0 = pl.multiple_of(c * CHUNK, CHUNK)
            gaps = gap_s[pl.ds(i0, CHUNK), :]

            def load(j):
                if j < 0 or j == rows:
                    side = 0 if j < 0 else 1
                    ph = halo[side, 0, pl.ds(i0, CHUNK), :].astype(F32)
                    co = halo[side, 1, pl.ds(i0, CHUNK), :].astype(F32)
                else:
                    ph = row_of(ph_s, j, i0, CHUNK)
                    co = row_of(co_s, j, i0, CHUNK)
                return ph * co, co

            window = [load(low - 1), load(low)]
            for j in range(low, high):
                window.append(load(j + 1))
                numer = box(window[0][0] + window[1][0] + window[2][0])
                denom = box(window[0][1] + window[1][1] + window[2][1])
                window.pop(0)
                smooth = numer / denom
                mean = denom * (1.0 / 9.0)
                weight = (gaps[:, j:j + 1] * mean).astype(BF16)
                for d in range(n):
                    w_send[d, j, pl.ds(i0, CHUNK), :] = weight[:, d * LANES:(d + 1) * LANES]
                sm_s[j, pl.ds(i0, CHUNK), :] = smooth
            return 0

        lax.fori_loop(0, chunks, body, 0)

    mine = pl.ds(pl.multiple_of(me * count, count), count)

    def exchange(src, dst, sems, part, low, high):
        span = pl.ds(low, high - low)
        copies = []
        for k in range(n - 1, 0, -1):
            d = lax.rem(me + k, n)
            copy = remote(src.at[d, span], dst.at[span, mine, :], sems, (part, k), (d, my_row))
            copy.start()
            copies.append(copy)
        own = pltpu.make_async_copy(src.at[me, span], dst.at[span, mine, :], sems.at[0, part, 0])
        own.start()
        copies.append(own)
        return copies

    half = rows // 2
    pending = []
    smooth_rows(1, half)
    pending += exchange(w_send, w_all, w_sems, 0, 1, half)

    wait_pair(terrain_copies, h_halo)

    def box_terrain(take):
        here = take(height[...])
        above = take(h_halo[0])[rows - 1:]
        below = take(h_halo[1])[:1]
        vert = here + jnp.concatenate([above, here[:-1]], axis=0) + jnp.concatenate([here[1:], below], axis=0)
        return box(vert)

    terrain_box = box_terrain(lambda h: h)
    square_box = box_terrain(lambda h: h * h)

    def moments(c, _):
        start = pl.multiple_of(c * CHUNK * rows, CHUNK * rows)
        top = jnp.zeros((CHUNK, rows, LANES), F32)
        low = jnp.zeros((CHUNK, rows, LANES), F32)
        for t in range(tiles):
            cols = slice(t * LANES, (t + 1) * LANES)
            co = co_s[t, pl.ds(start, CHUNK * rows), :].reshape(CHUNK, rows, LANES)
            ph = ph_s[t, pl.ds(start, CHUNK * rows), :].reshape(CHUNK, rows, LANES)
            top += co * ph * terrain_box[None, :, cols]
            low += co * square_box[None, :, cols]
        mom[0, pl.ds(start, CHUNK * rows), :] = top.reshape(CHUNK * rows, LANES)
        mom[1, pl.ds(start, CHUNK * rows), :] = low.reshape(CHUNK * rows, LANES)
        return 0

    lax.fori_loop(0, chunks, moments, 0)

    def summed(index):
        total = mom[index, pl.ds(0, count, stride=rows), :]
        for j in range(1, rows):
            total += mom[index, pl.ds(j, count, stride=rows), :]
        if count < LANES:
            total = jnp.concatenate([total, jnp.zeros((LANES - count, LANES), F32)], axis=0)
        return jnp.sum(total.T, axis=0, keepdims=True)

    mom_all[my_row] = jnp.concatenate([summed(0), summed(1), jnp.zeros((6, LANES), F32)], axis=0)
    mom_copies = []
    for k in range(1, m):
        copy = remote(mom_all.at[my_row], mom_all.at[my_row], mom_sems, (k,), (me, lax.rem(my_row + k, m)))
        copy.start()
        mom_copies.append(copy)

    lax.fori_loop(0, chunks, take_edges, 0)
    edge_copies = start_pair(edge.at[0], edge.at[1], halo, halo_sems)
    smooth_rows(half, rows - 1)
    pending += exchange(w_send, w_all, w_sems, 1, half, rows - 1)

    date = lax.broadcasted_iota(jnp.int32, (KPAD, ifgs), 0)
    signs = (date == pairs[1:2, :]).astype(F32) - (date == pairs[0:1, :]).astype(F32)
    gt[...] = signs[:DPAD].astype(BF16)
    g[...] = signs.T.astype(BF16)
    vb[...] = jnp.zeros_like(vb)

    for copy in mom_copies:
        copy.wait()
    sums = mom_all[0]
    for k in range(1, m):
        sums = sums + mom_all[k]
    slope = sums[0:1, :] / sums[1:2, :]
    topo_out[...] = slope[:, :count]
    topo_s[...] = jnp.broadcast_to(slope, (LANES, LANES)).T

    def correct_rows(low, high):
        def body(c, _):
            i0 = pl.multiple_of(c * CHUNK, CHUNK)
            column = topo_s[pl.ds(i0, CHUNK), :]
            for j in range(low, high):
                for d in range(n):
                    cols = pl.ds(d * LANES, LANES)
                    value = sm_s[j, pl.ds(i0, CHUNK), cols] - column * height[j:j + 1, cols]
                    c_send[d, j, pl.ds(i0, CHUNK), :] = value.astype(BF16)
            return 0

        lax.fori_loop(0, chunks, body, 0)

    correct_rows(1, half)
    pending += exchange(c_send, c_all, c_sems, 0, 1, half)
    correct_rows(half, rows - 1)
    pending += exchange(c_send, c_all, c_sems, 1, half, rows - 1)
    wait_pair(edge_copies, halo)
    last = []
    for part, j in ((2, 0), (3, rows - 1)):
        smooth_rows(j, j + 1)
        last += exchange(w_send, w_all, w_sems, part, j, j + 1)
        correct_rows(j, j + 1)
        last += exchange(c_send, c_all, c_sems, part, j, j + 1)

    def back_project(u):
        high, low = split(u)
        return dot(gt[...], high) + dot(gt[...], low)

    def right_rows(q, _):
        u = jnp.concatenate(
            [w_all[2 * q + i].astype(F32) * c_all[2 * q + i].astype(F32) for i in range(2)], axis=1
        )
        b = back_project(u)
        for i in range(2):
            r_s[2 * q + i] = b[:, i * LANES:(i + 1) * LANES]
        return 0

    for copy in pending:
        copy.wait()
    lax.fori_loop(1, half - 1, right_rows, 0)
    for copy in last:
        copy.wait()
    right_rows(0, 0)
    right_rows(half - 1, 0)

    small = lax.broadcasted_iota(jnp.int32, (DPAD, LANES), 1)

    def start_halo(v, step):
        first_packed = jnp.zeros((DPAD, LANES), F32)
        last_packed = jnp.zeros((DPAD, LANES), F32)
        for j in range(rows):
            tile = v[j]
            first_packed = jnp.where(small == j, pltpu.roll(tile, j, 1) if j else tile, first_packed)
            last_packed = jnp.where(small == j, pltpu.roll(tile, j + 1, 1), last_packed)
        pack[step, 0] = v[0].astype(BF16)
        pack[step, 1] = v[rows - 1].astype(BF16)
        pack[step, 2] = first_packed.astype(BF16)
        pack[step, 3] = last_packed.astype(BF16)
        left, right = (lax.max(me - 1, 0), my_row), (lax.min(me + 1, n - 1), my_row)
        copies = (
            (has_up, remote(pack.at[step, 0], halo_row.at[step, 1], row_sems, (step, 0), up)),
            (has_down, remote(pack.at[step, 1], halo_row.at[step, 0], row_sems, (step, 1), down)),
            (has_left, remote(pack.at[step, 2], halo_col.at[step, 1], col_sems, (step, 0), left)),
            (has_right, remote(pack.at[step, 3], halo_col.at[step, 0], col_sems, (step, 1), right)),
        )
        for there, copy in copies:
            pl.when(there)(copy.start)
        return copies

    def wait_halo(copies, step):
        for there, copy in copies:
            pl.when(there)(copy.wait_send)
        for index, buffer in ((0, halo_row), (1, halo_col)):
            low_there, low_copy = copies[2 * index]
            high_there, high_copy = copies[2 * index + 1]
            for side, there, copy in ((0, low_there, high_copy), (1, high_there, low_copy)):
                pl.when(there)(copy.wait_recv)

                @pl.when(jnp.logical_not(there))
                def _(side=side, buffer=buffer):
                    buffer[step, side] = jnp.zeros((DPAD, LANES), BF16)

    def apply(v, target, step, middle):
        copies = start_halo(v, step)

        def body(q, _):
            high, low = split(jnp.concatenate([v[2 * q], v[2 * q + 1]], axis=1))
            vb[0, :DPAD, :] = high
            vb[1, :DPAD, :] = low
            diff = dot(g[...], vb[0]) + dot(g[...], vb[1])
            u = jnp.concatenate(
                [diff[:, i * LANES:(i + 1) * LANES] * w_all[2 * q + i].astype(F32) for i in range(2)], axis=1
            )
            image = back_project(u)
            for i in range(2):
                target[2 * q + i] = image[:, i * LANES:(i + 1) * LANES]
            return 0

        lax.fori_loop(0, half // 2, body, 0)
        middle()
        lax.fori_loop(half // 2, half, body, 0)
        for j in range(rows):
            here = v[j]
            around = jnp.where(small == 0, 0.0, pltpu.roll(here, 1, 1))
            around += jnp.where(small == LANES - 1, 0.0, pltpu.roll(here, LANES - 1, 1))
            if j:
                around += v[j - 1]
            if j < rows - 1:
                around += v[j + 1]
            spread = 4.0 * here - around
            target[j] = target[j] + SMOOTHING_WEIGHT * spread + RIDGE_WEIGHT * here
        wait_halo(copies, step)
        left_col, right_col = halo_col[step, 0].astype(F32), halo_col[step, 1].astype(F32)
        for j in range(rows):
            left_edge = pltpu.roll(left_col, LANES - j, 1) if j else left_col
            right_edge = pltpu.roll(right_col, LANES - 1 - j, 1)
            beside = jnp.where(small == 0, left_edge, jnp.where(small == LANES - 1, right_edge, 0.0))
            if j == 0:
                beside += halo_row[step, 0].astype(F32)
            if j == rows - 1:
                beside += halo_row[step, 1].astype(F32)
            target[j] = target[j] - SMOOTHING_WEIGHT * beside

    def fold(value):
        return jnp.sum(value, axis=0, keepdims=True)

    def reduce_first(step, parts):
        filled = list(parts) + [jnp.zeros((8 - len(parts), LANES), F32)]
        red_a[step, me] = jnp.concatenate(filled, axis=0)
        copies = []
        for k in range(1, n):
            copy = remote(red_a.at[step, me], red_a.at[step, me], a_sems, (step, k), (lax.rem(me + k, n), my_row))
            copy.start()
            copies.append(copy)
        return copies

    def reduce_second(step, copies):
        for copy in copies:
            copy.wait()
        total = red_a[step, 0]
        for k in range(1, n):
            total = total + red_a[step, k]
        red_b[step, my_row] = total
        later = []
        for k in range(1, m):
            copy = remote(red_b.at[step, my_row], red_b.at[step, my_row], b_sems, (step, k), (me, lax.rem(my_row + k, m)))
            copy.start()
            later.append(copy)
        return later

    def reduce_last(step, copies):
        for copy in copies:
            copy.wait()
        total = red_b[step, 0]
        for k in range(1, m):
            total = total + red_b[step, k]
        total = jnp.sum(total, axis=1, keepdims=True)
        return [total[i:i + 1, :] for i in range(3)]

    def overlapped(step, parts, v, target, apply_step):
        state = {"copies": reduce_first(step, parts)}

        def middle():
            state["copies"] = reduce_second(step, state["copies"])

        apply(v, target, apply_step, middle)
        return reduce_last(step, state["copies"])

    apply(r_s, w_s, 0, lambda: None)
    gamma_sum = jnp.zeros((1, LANES), F32)
    delta_sum = jnp.zeros((1, LANES), F32)
    for j in range(rows):
        gamma_sum += fold(r_s[j] * r_s[j])
        delta_sum += fold(r_s[j] * w_s[j])
    gamma, curve, _ = overlapped(0, (gamma_sum, delta_sum), w_s, n_s, 1)

    alpha = gamma / curve
    alpha_first = alpha
    gamma_sum = jnp.zeros((1, LANES), F32)
    delta_sum = jnp.zeros((1, LANES), F32)
    cross_sum = jnp.zeros((1, LANES), F32)
    for j in range(rows):
        p, s, z = r_s[j], w_s[j], n_s[j]
        r = p - alpha * s
        w = s - alpha * z
        p_s[j], s_s[j], z_s[j] = p, s, z
        r_s[j], w_s[j] = r, w
        gamma_sum += fold(r * r)
        delta_sum += fold(r * w)
        cross_sum += fold(r * s)
    gamma_next, delta, cross = overlapped(1, (gamma_sum, delta_sum, cross_sum), w_s, n_s, 2)

    beta = gamma_next / gamma
    gamma = gamma_next
    curve = delta + 2.0 * beta * cross + beta * beta * curve
    alpha = gamma / curve
    gamma_sum = jnp.zeros((1, LANES), F32)
    delta_sum = jnp.zeros((1, LANES), F32)
    cross_sum = jnp.zeros((1, LANES), F32)
    for j in range(rows):
        r, w = r_s[j], w_s[j]
        first_p = p_s[j]
        p = r + beta * first_p
        s = w + beta * s_s[j]
        z = n_s[j] + beta * z_s[j]
        r = r - alpha * s
        w = w - alpha * z
        p_s[j] = p
        r_s[j] = r
        z_s[j] = alpha_first * first_p + alpha * p
        gamma_sum += fold(r * r)
        delta_sum += fold(r * w)
        cross_sum += fold(r * s)
    copies = reduce_first(2, (gamma_sum, delta_sum, cross_sum))
    gamma_next, delta, cross = reduce_last(2, reduce_second(2, copies))
    beta = gamma_next / gamma
    curve = delta + 2.0 * beta * cross + beta * beta * curve
    alpha = gamma_next / curve
    for j in range(rows):
        x = z_s[j] + alpha * (r_s[j] + beta * p_s[j])
        out[pl.ds(j, DATES, stride=rows), :] = x[:DATES]


def solution(mesh):
    n, m = mesh.shape["ifg"], mesh.shape["rows"]

    def per_device(phase, coherence, height, gap_mask, date_pairs):
        count, rows, width = phase.shape
        ifgs = date_pairs.shape[0]
        tiles = width // LANES
        dma = pltpu.SemaphoreType.DMA
        state = pltpu.VMEM((rows, DPAD, LANES), F32)
        vmem = pl.BlockSpec(memory_space=pltpu.VMEM)
        displacement, topo = pl.pallas_call(
            functools.partial(kernel, n, m),
            out_shape=(
                jax.ShapeDtypeStruct((DATES * rows, LANES), F32),
                jax.ShapeDtypeStruct((1, count), F32),
            ),
            in_specs=[vmem] * 5,
            out_specs=(vmem, vmem),
            scratch_shapes=[
                pltpu.VMEM((tiles, count * rows, LANES), F32),
                pltpu.VMEM((tiles, count * rows, LANES), F32),
                pltpu.VMEM((2, 2, count, width), BF16),
                pltpu.VMEM((2, 2, count, width), BF16),
                pltpu.VMEM((rows, count, width), F32),
                pltpu.VMEM((n, rows, count, LANES), BF16),
                pltpu.VMEM((rows, ifgs, LANES), BF16),
                pltpu.VMEM((n, rows, count, LANES), BF16),
                pltpu.VMEM((rows, ifgs, LANES), BF16),
                pltpu.VMEM((2, rows, width), F32),
                pltpu.VMEM((count, rows), F32),
                pltpu.VMEM((2, count * rows, LANES), F32),
                pltpu.VMEM((m, 8, LANES), F32),
                pltpu.VMEM((LANES, LANES), F32),
                pltpu.VMEM((ifgs, KPAD), BF16),
                pltpu.VMEM((DPAD, ifgs), BF16),
                pltpu.VMEM((2, KPAD, 2 * LANES), BF16),
                state, state, state, state, state, state,
                pltpu.VMEM((3, 4, DPAD, LANES), BF16),
                pltpu.VMEM((3, 2, DPAD, LANES), BF16),
                pltpu.VMEM((3, 2, DPAD, LANES), BF16),
                pltpu.VMEM((3, n, 8, LANES), F32),
                pltpu.VMEM((3, m, 8, LANES), F32),
                dma((2, 2)),
                dma((2, 2)),
                dma((2, 4, n)),
                dma((2, 4, n)),
                dma((2, m)),
                dma((2, 3, 2)),
                dma((2, 3, 2)),
                dma((2, 3, n)),
                dma((2, 3, m)),
            ],
            compiler_params=pltpu.CompilerParams(
                collective_id=0, has_side_effects=True, vmem_limit_bytes=56 * 1024 * 1024
            ),
        )(phase, coherence, height, gap_mask.T, date_pairs.T)
        return displacement.reshape(DATES, rows, LANES), topo.reshape(count)

    return jax.shard_map(
        per_device,
        mesh=mesh,
        in_specs=(
            P("ifg", "rows", None),
            P("ifg", "rows", None),
            P("rows", None),
            P("ifg", "rows"),
            P(),
        ),
        out_specs=(P(None, "rows", "ifg"), P("ifg")),
        check_vma=False,
    )
```

```python
import functools

import jax
import jax.numpy as jnp
from jax import lax
from jax.experimental import pallas as pl
from jax.experimental.pallas import tpu as pltpu
from jax.sharding import PartitionSpec as P

DATES = 300
DPAD = 304
KPAD = 640
LANES = 128
CHUNK = 16
BLOCK = 104
SMOOTHING_WEIGHT = 0.5
RIDGE_WEIGHT = 0.05
F32 = jnp.float32
BF16 = jnp.bfloat16
MESH = pl.DeviceIdType.MESH


def split(value):
    high = value.astype(BF16)
    low = (value - high.astype(F32)).astype(BF16)
    return high, low


def dot(a, b):
    return jnp.dot(a, b, preferred_element_type=F32)


def kernel(
    n, m,
    phase, coher, height, gap, pairs,
    x_out, topo_out,
    ph_s, co_s, edge, halo, sm_s, w_send, w_all, c_send, c_all,
    h_halo, gap_s, mom, mom_all, topo_s, g, gt,
    r_s, w_s, n_s, p_s, s_s, z_s,
    pack, halo_row, halo_col, red_a, red_b,
    h_sems, halo_sems, w_sems, c_sems, mom_sems, row_sems, col_sems, a_sems, b_sems,
):
    count, rows, width = phase.shape
    ifgs = pairs.shape[1]
    tiles = width // LANES
    chunks = count // CHUNK
    me = lax.axis_index("ifg")
    my_row = lax.axis_index("rows")
    has_up, has_down = my_row > 0, my_row < m - 1
    has_left, has_right = me > 0, me < n - 1

    barrier = pltpu.get_barrier_semaphore()
    for k in range(1, n):
        pl.semaphore_signal(barrier, inc=1, device_id=(lax.rem(me + k, n), my_row), device_id_type=MESH)
    for k in range(1, m):
        pl.semaphore_signal(barrier, inc=1, device_id=(me, lax.rem(my_row + k, m)), device_id_type=MESH)

    def remote(src, dst, sems, index, target):
        return pltpu.make_async_remote_copy(
            src_ref=src, dst_ref=dst,
            send_sem=sems.at[(0,) + index], recv_sem=sems.at[(1,) + index],
            device_id=target, device_id_type=MESH,
        )

    def widen(c, _):
        for src, dst in ((phase, ph_s), (coher, co_s)):
            block = src[pl.ds(c * CHUNK, CHUNK)].astype(F32).reshape(CHUNK * rows, width)
            for t in range(tiles):
                dst[t, pl.ds(pl.multiple_of(c * CHUNK * rows, CHUNK * rows), CHUNK * rows), :] = (
                    block[:, t * LANES:(t + 1) * LANES]
                )
        return 0

    lax.fori_loop(0, chunks, widen, 0)

    def row_of(ref, j, i0, size):
        return jnp.concatenate(
            [ref[t, pl.ds(i0 * rows + j, size, stride=rows), :] for t in range(tiles)], axis=1
        )

    gap_s[...] = gap[...].astype(F32).T
    pl.semaphore_wait(barrier, n + m - 2)
    up, down = (me, lax.max(my_row - 1, 0)), (me, lax.min(my_row + 1, m - 1))

    def start_pair(sent_up, sent_down, landing, sems):
        to_up = remote(sent_up, landing.at[1], sems, (0,), up)
        to_down = remote(sent_down, landing.at[0], sems, (1,), down)
        pl.when(has_up)(to_up.start)
        pl.when(has_down)(to_down.start)
        return to_up, to_down

    def wait_pair(copies, landing):
        to_up, to_down = copies
        for there, sent, received, side in ((has_up, to_up, to_down, 0), (has_down, to_down, to_up, 1)):
            pl.when(there)(sent.wait_send)
            pl.when(there)(received.wait_recv)

            @pl.when(jnp.logical_not(there))
            def _(side=side):
                landing[side] = jnp.zeros_like(landing[side])

    terrain_copies = start_pair(height, height, h_halo, h_sems)

    def take_edges(c, _):
        i0 = pl.multiple_of(c * CHUNK, CHUNK)
        for side, j in ((0, 0), (1, rows - 1)):
            for a, ref in ((0, ph_s), (1, co_s)):
                edge[side, a, pl.ds(i0, CHUNK), :] = row_of(ref, j, i0, CHUNK).astype(BF16)
        return 0


    def box(vert):
        lane = lax.broadcasted_iota(jnp.int32, vert.shape, 1)
        before = jnp.where(lane == 0, 0.0, pltpu.roll(vert, 1, 1))
        after = jnp.where(lane == width - 1, 0.0, pltpu.roll(vert, width - 1, 1))
        return vert + before + after

    def smooth_rows(low, high):
        def body(c, _):
            i0 = pl.multiple_of(c * CHUNK, CHUNK)
            gaps = gap_s[pl.ds(i0, CHUNK), :]

            def load(j):
                if j < 0 or j == rows:
                    side = 0 if j < 0 else 1
                    ph = halo[side, 0, pl.ds(i0, CHUNK), :].astype(F32)
                    co = halo[side, 1, pl.ds(i0, CHUNK), :].astype(F32)
                else:
                    ph = row_of(ph_s, j, i0, CHUNK)
                    co = row_of(co_s, j, i0, CHUNK)
                return ph * co, co

            window = [load(low - 1), load(low)]
            for j in range(low, high):
                window.append(load(j + 1))
                numer = box(window[0][0] + window[1][0] + window[2][0])
                denom = box(window[0][1] + window[1][1] + window[2][1])
                window.pop(0)
                smooth = numer / denom
                mean = denom * (1.0 / 9.0)
                weight = (gaps[:, j:j + 1] * mean).astype(BF16)
                for d in range(n):
                    w_send[d, j, pl.ds(i0, CHUNK), :] = weight[:, d * LANES:(d + 1) * LANES]
                sm_s[j, pl.ds(i0, CHUNK), :] = smooth
            return 0

        lax.fori_loop(0, chunks, body, 0)

    mine = pl.ds(pl.multiple_of(me * count, count), count)

    def exchange(src, dst, sems, part, low, high):
        span = pl.ds(low, high - low)
        copies = []
        for k in range(n - 1, 0, -1):
            d = lax.rem(me + k, n)
            copy = remote(src.at[d, span], dst.at[span, mine, :], sems, (part, k), (d, my_row))
            copy.start()
            copies.append(copy)
        own = pltpu.make_async_copy(src.at[me, span], dst.at[span, mine, :], sems.at[0, part, 0])
        own.start()
        copies.append(own)
        return copies

    half = rows // 2
    smooth_rows(1, 3)
    w_copies = [exchange(w_send, w_all, w_sems, 0, 1, 3)]

    wait_pair(terrain_copies, h_halo)

    def box_terrain(take):
        here = take(height[...])
        above = take(h_halo[0])[rows - 1:]
        below = take(h_halo[1])[:1]
        vert = here + jnp.concatenate([above, here[:-1]], axis=0) + jnp.concatenate([here[1:], below], axis=0)
        return box(vert)

    terrain_box = box_terrain(lambda h: h)
    square_box = box_terrain(lambda h: h * h)

    def moments(c, _):
        start = pl.multiple_of(c * CHUNK * rows, CHUNK * rows)
        top = jnp.zeros((CHUNK, rows, LANES), F32)
        low = jnp.zeros((CHUNK, rows, LANES), F32)
        for t in range(tiles):
            cols = slice(t * LANES, (t + 1) * LANES)
            co = co_s[t, pl.ds(start, CHUNK * rows), :].reshape(CHUNK, rows, LANES)
            ph = ph_s[t, pl.ds(start, CHUNK * rows), :].reshape(CHUNK, rows, LANES)
            top += co * ph * terrain_box[None, :, cols]
            low += co * square_box[None, :, cols]
        mom[0, pl.ds(start, CHUNK * rows), :] = top.reshape(CHUNK * rows, LANES)
        mom[1, pl.ds(start, CHUNK * rows), :] = low.reshape(CHUNK * rows, LANES)
        return 0

    lax.fori_loop(0, chunks, moments, 0)

    def summed(index):
        total = mom[index, pl.ds(0, count, stride=rows), :]
        for j in range(1, rows):
            total += mom[index, pl.ds(j, count, stride=rows), :]
        if count < LANES:
            total = jnp.concatenate([total, jnp.zeros((LANES - count, LANES), F32)], axis=0)
        return jnp.sum(total.T, axis=0, keepdims=True)

    mom_all[my_row] = jnp.concatenate([summed(0), summed(1), jnp.zeros((6, LANES), F32)], axis=0)
    mom_copies = []
    for k in range(1, m):
        copy = remote(mom_all.at[my_row], mom_all.at[my_row], mom_sems, (k,), (me, lax.rem(my_row + k, m)))
        copy.start()
        mom_copies.append(copy)

    lax.fori_loop(0, chunks, take_edges, 0)
    edge_copies = start_pair(edge.at[0], edge.at[1], halo, halo_sems)
    for q in range(1, half - 1):
        smooth_rows(2 * q + 1, 2 * q + 3)
        w_copies.append(exchange(w_send, w_all, w_sems, q, 2 * q + 1, 2 * q + 3))

    date = lax.broadcasted_iota(jnp.int32, (KPAD, ifgs), 0)
    date = jnp.where(date >= DPAD, date - DPAD, date)
    signs = (date == pairs[1:2, :]).astype(F32) - (date == pairs[0:1, :]).astype(F32)
    gt[:, :ifgs] = signs[:DPAD].astype(BF16)
    gt[:, ifgs:] = signs[:DPAD].astype(BF16)
    g[...] = signs.T.astype(BF16)

    for copy in mom_copies:
        copy.wait()
    sums = mom_all[0]
    for k in range(1, m):
        sums = sums + mom_all[k]
    slope = sums[0:1, :] / sums[1:2, :]
    topo_out[...] = slope[:, :count]
    topo_s[...] = jnp.broadcast_to(slope, (LANES, LANES)).T

    def correct_rows(low, high):
        def body(c, _):
            i0 = pl.multiple_of(c * CHUNK, CHUNK)
            column = topo_s[pl.ds(i0, CHUNK), :]
            for j in range(low, high):
                for d in range(n):
                    cols = pl.ds(d * LANES, LANES)
                    value = sm_s[j, pl.ds(i0, CHUNK), cols] - column * height[j:j + 1, cols]
                    c_send[d, j, pl.ds(i0, CHUNK), :] = value.astype(BF16)
            return 0

        lax.fori_loop(0, chunks, body, 0)

    c_copies = []
    for q in range(half - 1):
        correct_rows(2 * q + 1, 2 * q + 3)
        c_copies.append(exchange(c_send, c_all, c_sems, q, 2 * q + 1, 2 * q + 3))
    wait_pair(edge_copies, halo)
    last = []
    for part, j in ((half - 1, rows - 1), (half, 0)):
        smooth_rows(j, j + 1)
        last += exchange(w_send, w_all, w_sems, part, j, j + 1)
        correct_rows(j, j + 1)
        last += exchange(c_send, c_all, c_sems, part, j, j + 1)

    def pair(q):
        return 2 * q + 1, (2 * q + 2) % rows

    def both(q, of):
        return jnp.concatenate([of(j) for j in pair(q)], axis=1)

    def put(target, q, value):
        for i, j in enumerate(pair(q)):
            target[j] = value[:, i * LANES:(i + 1) * LANES]

    def back_project(u):
        return dot(gt[...], jnp.concatenate(split(u), axis=0))

    def right_rows(q):
        put(r_s, q, back_project(both(q, lambda j: w_all[j].astype(F32) * c_all[j].astype(F32))))

    def weighted(v, target, q):
        high, low = split(both(q, lambda j: v[j]))
        filler = jnp.zeros((KPAD - 2 * DPAD, 2 * LANES), BF16)
        diff = dot(g[...], jnp.concatenate([high, low, filler], axis=0))
        put(target, q, back_project(diff * both(q, lambda j: w_all[j].astype(F32))))

    small = lax.broadcasted_iota(jnp.int32, (DPAD, LANES), 1)

    def start_halo(v, step):
        first_packed = jnp.zeros((DPAD, LANES), F32)
        last_packed = jnp.zeros((DPAD, LANES), F32)
        for j in range(rows):
            tile = v[j]
            first_packed = jnp.where(small == j, pltpu.roll(tile, j, 1) if j else tile, first_packed)
            last_packed = jnp.where(small == j, pltpu.roll(tile, j + 1, 1), last_packed)
        pack[step, 0] = v[0].astype(BF16)
        pack[step, 1] = v[rows - 1].astype(BF16)
        pack[step, 2] = first_packed.astype(BF16)
        pack[step, 3] = last_packed.astype(BF16)
        left, right = (lax.max(me - 1, 0), my_row), (lax.min(me + 1, n - 1), my_row)
        copies = (
            (has_up, remote(pack.at[step, 0], halo_row.at[step, 1], row_sems, (step, 0), up)),
            (has_down, remote(pack.at[step, 1], halo_row.at[step, 0], row_sems, (step, 1), down)),
            (has_left, remote(pack.at[step, 2], halo_col.at[step, 1], col_sems, (step, 0), left)),
            (has_right, remote(pack.at[step, 3], halo_col.at[step, 0], col_sems, (step, 1), right)),
        )
        for there, copy in copies:
            pl.when(there)(copy.start)
        return copies

    def wait_halo(copies, step):
        for there, copy in copies:
            pl.when(there)(copy.wait_send)
        for index, buffer in ((0, halo_row), (1, halo_col)):
            low_there, low_copy = copies[2 * index]
            high_there, high_copy = copies[2 * index + 1]
            for side, there, copy in ((0, low_there, high_copy), (1, high_there, low_copy)):
                pl.when(there)(copy.wait_recv)

                @pl.when(jnp.logical_not(there))
                def _(side=side, buffer=buffer):
                    buffer[step, side] = jnp.zeros((DPAD, LANES), BF16)

    def spread_and_halo(v, target, step, copies):
        for j in range(rows):
            here = v[j]
            around = jnp.where(small == 0, 0.0, pltpu.roll(here, 1, 1))
            around += jnp.where(small == LANES - 1, 0.0, pltpu.roll(here, LANES - 1, 1))
            if j:
                around += v[j - 1]
            if j < rows - 1:
                around += v[j + 1]
            spread = 4.0 * here - around
            target[j] = target[j] + SMOOTHING_WEIGHT * spread + RIDGE_WEIGHT * here
        wait_halo(copies, step)
        left_col, right_col = halo_col[step, 0].astype(F32), halo_col[step, 1].astype(F32)
        for j in range(rows):
            left_edge = pltpu.roll(left_col, LANES - j, 1) if j else left_col
            right_edge = pltpu.roll(right_col, LANES - 1 - j, 1)
            beside = jnp.where(small == 0, left_edge, jnp.where(small == LANES - 1, right_edge, 0.0))
            if j == 0:
                beside += halo_row[step, 0].astype(F32)
            if j == rows - 1:
                beside += halo_row[step, 1].astype(F32)
            target[j] = target[j] - SMOOTHING_WEIGHT * beside

    def apply(v, target, step, middle):
        copies = start_halo(v, step)
        for q in range(half):
            weighted(v, target, q)
            if q == half // 2 - 1:
                middle()
        spread_and_halo(v, target, step, copies)

    def fold(value):
        return jnp.sum(value, axis=0, keepdims=True)

    def reduce_first(step, parts):
        filled = list(parts) + [jnp.zeros((8 - len(parts), LANES), F32)]
        red_a[step, me] = jnp.concatenate(filled, axis=0)
        copies = []
        for k in range(1, n):
            copy = remote(red_a.at[step, me], red_a.at[step, me], a_sems, (step, k), (lax.rem(me + k, n), my_row))
            copy.start()
            copies.append(copy)
        return copies

    def reduce_second(step, copies):
        for copy in copies:
            copy.wait()
        total = red_a[step, 0]
        for k in range(1, n):
            total = total + red_a[step, k]
        red_b[step, my_row] = total
        later = []
        for k in range(1, m):
            copy = remote(red_b.at[step, my_row], red_b.at[step, my_row], b_sems, (step, k), (me, lax.rem(my_row + k, m)))
            copy.start()
            later.append(copy)
        return later

    def reduce_last(step, copies):
        for copy in copies:
            copy.wait()
        total = red_b[step, 0]
        for k in range(1, m):
            total = total + red_b[step, k]
        total = jnp.sum(total, axis=1, keepdims=True)
        return [total[i:i + 1, :] for i in range(3)]

    def overlapped(step, parts, v, target, apply_step):
        state = {"copies": reduce_first(step, parts)}

        def middle():
            state["copies"] = reduce_second(step, state["copies"])

        apply(v, target, apply_step, middle)
        return reduce_last(step, state["copies"])

    for q in range(half - 1):
        for copy in w_copies[q] + c_copies[q]:
            copy.wait()
        right_rows(q)
        weighted(r_s, w_s, q)
    for copy in last:
        copy.wait()
    right_rows(half - 1)
    copies = start_halo(r_s, 0)
    weighted(r_s, w_s, half - 1)
    spread_and_halo(r_s, w_s, 0, copies)
    gamma_sum = jnp.zeros((1, LANES), F32)
    delta_sum = jnp.zeros((1, LANES), F32)
    for j in range(rows):
        gamma_sum += fold(r_s[j] * r_s[j])
        delta_sum += fold(r_s[j] * w_s[j])
    gamma, curve, _ = overlapped(0, (gamma_sum, delta_sum), w_s, n_s, 1)

    alpha = gamma / curve
    alpha_first = alpha
    gamma_sum = jnp.zeros((1, LANES), F32)
    delta_sum = jnp.zeros((1, LANES), F32)
    cross_sum = jnp.zeros((1, LANES), F32)
    for j in range(rows):
        p, s, z = r_s[j], w_s[j], n_s[j]
        r = p - alpha * s
        w = s - alpha * z
        p_s[j], s_s[j], z_s[j] = p, s, z
        r_s[j], w_s[j] = r, w
        gamma_sum += fold(r * r)
        delta_sum += fold(r * w)
        cross_sum += fold(r * s)
    gamma_next, delta, cross = overlapped(1, (gamma_sum, delta_sum, cross_sum), w_s, n_s, 2)

    beta = gamma_next / gamma
    gamma = gamma_next
    curve = delta + 2.0 * beta * cross + beta * beta * curve
    alpha = gamma / curve
    gamma_sum = jnp.zeros((1, LANES), F32)
    delta_sum = jnp.zeros((1, LANES), F32)
    cross_sum = jnp.zeros((1, LANES), F32)
    for j in range(rows):
        r, w = r_s[j], w_s[j]
        first_p = p_s[j]
        p = r + beta * first_p
        s = w + beta * s_s[j]
        z = n_s[j] + beta * z_s[j]
        r = r - alpha * s
        w = w - alpha * z
        p_s[j] = p
        r_s[j] = r
        z_s[j] = alpha_first * first_p + alpha * p
        gamma_sum += fold(r * r)
        delta_sum += fold(r * w)
        cross_sum += fold(r * s)
    copies = reduce_first(2, (gamma_sum, delta_sum, cross_sum))
    gamma_next, delta, cross = reduce_last(2, reduce_second(2, copies))
    beta = gamma_next / gamma
    curve = delta + 2.0 * beta * cross + beta * beta * curve
    alpha = gamma_next / curve
    for j in range(rows):
        x_out[j] = z_s[j] + alpha * (r_s[j] + beta * p_s[j])


def order_dates(x, topo, out, topo_out):
    rows, dates, _ = x.shape
    for j in range(rows):
        out[pl.ds(j, dates, stride=rows), :] = x[j]
    topo_out[...] = topo[...]


def solution(mesh):
    n, m = mesh.shape["ifg"], mesh.shape["rows"]

    def per_device(phase, coherence, height, gap_mask, date_pairs):
        count, rows, width = phase.shape
        ifgs = date_pairs.shape[0]
        tiles = width // LANES
        dma = pltpu.SemaphoreType.DMA
        state = pltpu.VMEM((rows, DPAD, LANES), F32)
        vmem = pl.BlockSpec(memory_space=pltpu.VMEM)
        field, topo = pl.pallas_call(
            functools.partial(kernel, n, m),
            out_shape=(
                jax.ShapeDtypeStruct((rows, DPAD, LANES), F32),
                jax.ShapeDtypeStruct((1, count), F32),
            ),
            in_specs=[vmem] * 5,
            out_specs=(vmem, vmem),
            scratch_shapes=[
                pltpu.VMEM((tiles, count * rows, LANES), F32),
                pltpu.VMEM((tiles, count * rows, LANES), F32),
                pltpu.VMEM((2, 2, count, width), BF16),
                pltpu.VMEM((2, 2, count, width), BF16),
                pltpu.VMEM((rows, count, width), F32),
                pltpu.VMEM((n, rows, count, LANES), BF16),
                pltpu.VMEM((rows, ifgs, LANES), BF16),
                pltpu.VMEM((n, rows, count, LANES), BF16),
                pltpu.VMEM((rows, ifgs, LANES), BF16),
                pltpu.VMEM((2, rows, width), F32),
                pltpu.VMEM((count, rows), F32),
                pltpu.VMEM((2, count * rows, LANES), F32),
                pltpu.VMEM((m, 8, LANES), F32),
                pltpu.VMEM((LANES, LANES), F32),
                pltpu.VMEM((ifgs, KPAD), BF16),
                pltpu.VMEM((DPAD, 2 * ifgs), BF16),
                state, state, state, state, state, state,
                pltpu.VMEM((3, 4, DPAD, LANES), BF16),
                pltpu.VMEM((3, 2, DPAD, LANES), BF16),
                pltpu.VMEM((3, 2, DPAD, LANES), BF16),
                pltpu.VMEM((3, n, 8, LANES), F32),
                pltpu.VMEM((3, m, 8, LANES), F32),
                dma((2, 2)),
                dma((2, 2)),
                dma((2, rows // 2 + 1, n)),
                dma((2, rows // 2 + 1, n)),
                dma((2, m)),
                dma((2, 3, 2)),
                dma((2, 3, 2)),
                dma((2, 3, n)),
                dma((2, 3, m)),
            ],
            compiler_params=pltpu.CompilerParams(
                collective_id=0, has_side_effects=True, vmem_limit_bytes=56 * 1024 * 1024
            ),
        )(phase, coherence, height, gap_mask.T, date_pairs.T)
        displacement, topo = pl.pallas_call(
            order_dates,
            grid=(pl.cdiv(DATES, BLOCK),),
            out_shape=(
                jax.ShapeDtypeStruct((DATES * rows, LANES), F32),
                jax.ShapeDtypeStruct((1, count), F32),
            ),
            in_specs=[
                pl.BlockSpec((rows, BLOCK, LANES), lambda i: (0, i, 0)),
                pl.BlockSpec((1, count), lambda i: (0, 0)),
            ],
            out_specs=(
                pl.BlockSpec((BLOCK * rows, LANES), lambda i: (i, 0)),
                pl.BlockSpec((1, count), lambda i: (0, 0)),
            ),
        )(field, topo)
        return displacement.reshape(DATES, rows, LANES), topo.reshape(count)

    return jax.shard_map(
        per_device,
        mesh=mesh,
        in_specs=(
            P("ifg", "rows", None),
            P("ifg", "rows", None),
            P("rows", None),
            P("ifg", "rows"),
            P(),
        ),
        out_specs=(P(None, "rows", "ifg"), P("ifg")),
        check_vma=False,
    )
```

```python
import functools

import jax
import jax.numpy as jnp
from jax import lax
from jax.experimental import pallas as pl
from jax.experimental.pallas import tpu as pltpu
from jax.sharding import PartitionSpec as P

DATES = 300
DPAD = 304
KPAD = 640
LANES = 128
CHUNK = 16
BLOCK = 104
SMOOTHING_WEIGHT = 0.5
RIDGE_WEIGHT = 0.05
F32 = jnp.float32
BF16 = jnp.bfloat16
MESH = pl.DeviceIdType.MESH


def split(value):
    high = value.astype(BF16)
    low = (value - high.astype(F32)).astype(BF16)
    return high, low


def dot(a, b):
    return jnp.dot(a, b, preferred_element_type=F32)


def kernel(
    n, m,
    phase, coher, height, gap, pairs,
    x_out, topo_out,
    halo, sm_s, w_send, w_all, c_send, c_all,
    h_halo, gap_s, mom, mom_all, topo_s, g, gt, pick, place,
    r_s, w_s, n_s, p_s, s_s, z_s,
    pack, halo_row, halo_col, red_a, red_b,
    h_sems, halo_sems, w_sems, c_sems, mom_sems, row_sems, col_sems, a_sems, b_sems,
):
    rows, count, width = phase.shape
    ifgs = pairs.shape[1]
    tiles = width // LANES
    chunks = count // CHUNK
    me = lax.axis_index("ifg")
    my_row = lax.axis_index("rows")
    has_up, has_down = my_row > 0, my_row < m - 1
    has_left, has_right = me > 0, me < n - 1

    barrier = pltpu.get_barrier_semaphore()
    for k in range(1, n):
        pl.semaphore_signal(barrier, inc=1, device_id=(lax.rem(me + k, n), my_row), device_id_type=MESH)
    for k in range(1, m):
        pl.semaphore_signal(barrier, inc=1, device_id=(me, lax.rem(my_row + k, m)), device_id_type=MESH)

    def remote(src, dst, sems, index, target):
        return pltpu.make_async_remote_copy(
            src_ref=src, dst_ref=dst,
            send_sem=sems.at[(0,) + index], recv_sem=sems.at[(1,) + index],
            device_id=target, device_id_type=MESH,
        )

    gap_s[...] = gap[...].astype(F32).T
    pl.semaphore_wait(barrier, n + m - 2)
    up, down = (me, lax.max(my_row - 1, 0)), (me, lax.min(my_row + 1, m - 1))

    def start_pair(sent_up, sent_down, landing, sems):
        to_up = remote(sent_up, landing.at[1], sems, (0,), up)
        to_down = remote(sent_down, landing.at[0], sems, (1,), down)
        pl.when(has_up)(to_up.start)
        pl.when(has_down)(to_down.start)
        return to_up, to_down

    def wait_pair(copies, landing):
        to_up, to_down = copies
        for there, sent, received, side in ((has_up, to_up, to_down, 0), (has_down, to_down, to_up, 1)):
            pl.when(there)(sent.wait_send)
            pl.when(there)(received.wait_recv)

            @pl.when(jnp.logical_not(there))
            def _(side=side):
                landing[side] = jnp.zeros_like(landing[side])

    terrain_copies = start_pair(height, height, h_halo, h_sems)

    def box(vert):
        lane = lax.broadcasted_iota(jnp.int32, vert.shape, 1)
        before = jnp.where(lane == 0, 0.0, pltpu.roll(vert, 1, 1))
        after = jnp.where(lane == width - 1, 0.0, pltpu.roll(vert, width - 1, 1))
        return vert + before + after

    def smooth_rows(low, high):
        def body(c, _):
            i0 = pl.multiple_of(c * CHUNK, CHUNK)
            gaps = gap_s[pl.ds(i0, CHUNK), :]

            def load(j):
                if j < 0 or j == rows:
                    side = 0 if j < 0 else 1
                    ph = halo[0, side, pl.ds(i0, CHUNK), :].astype(F32)
                    co = halo[1, side, pl.ds(i0, CHUNK), :].astype(F32)
                else:
                    ph = phase[j, pl.ds(i0, CHUNK), :].astype(F32)
                    co = coher[j, pl.ds(i0, CHUNK), :].astype(F32)
                return ph * co, co

            window = [load(low - 1), load(low)]
            for j in range(low, high):
                window.append(load(j + 1))
                numer = box(window[0][0] + window[1][0] + window[2][0])
                denom = box(window[0][1] + window[1][1] + window[2][1])
                window.pop(0)
                smooth = numer / denom
                mean = denom * (1.0 / 9.0)
                weight = (gaps[:, j:j + 1] * mean).astype(BF16)
                for d in range(n):
                    w_send[d, j, pl.ds(i0, CHUNK), :] = weight[:, d * LANES:(d + 1) * LANES]
                sm_s[j, pl.ds(i0, CHUNK), :] = smooth
            return 0

        lax.fori_loop(0, chunks, body, 0)

    mine = pl.ds(pl.multiple_of(me * count, count), count)

    def exchange(src, dst, sems, part, low, high):
        span = pl.ds(low, high - low)
        copies = []
        for k in range(n - 1, 0, -1):
            d = lax.rem(me + k, n)
            copy = remote(src.at[d, span], dst.at[span, mine, :], sems, (part, k), (d, my_row))
            copy.start()
            copies.append(copy)
        own = pltpu.make_async_copy(src.at[me, span], dst.at[span, mine, :], sems.at[0, part, 0])
        own.start()
        copies.append(own)
        return copies

    half = rows // 2
    smooth_rows(1, 3)
    w_copies = [exchange(w_send, w_all, w_sems, 0, 1, 3)]

    wait_pair(terrain_copies, h_halo)

    def box_terrain(take):
        here = take(height[...])
        above = take(h_halo[0])[rows - 1:]
        below = take(h_halo[1])[:1]
        vert = here + jnp.concatenate([above, here[:-1]], axis=0) + jnp.concatenate([here[1:], below], axis=0)
        return box(vert)

    terrain_box = box_terrain(lambda h: h)
    square_box = box_terrain(lambda h: h * h)

    if count < LANES:
        mom[...] = jnp.zeros_like(mom)

    def moments(c, _):
        i0 = pl.multiple_of(c * CHUNK, CHUNK)
        top = jnp.zeros((CHUNK, LANES), F32)
        low = jnp.zeros((CHUNK, LANES), F32)
        for j in range(rows):
            co = coher[j, pl.ds(i0, CHUNK), :].astype(F32)
            ph = phase[j, pl.ds(i0, CHUNK), :].astype(F32)
            first = co * ph * terrain_box[j:j + 1, :]
            second = co * square_box[j:j + 1, :]
            for t in range(tiles):
                cols = slice(t * LANES, (t + 1) * LANES)
                top += first[:, cols]
                low += second[:, cols]
        mom[0, pl.ds(i0, CHUNK), :] = top
        mom[1, pl.ds(i0, CHUNK), :] = low
        return 0

    lax.fori_loop(0, chunks, moments, 0)

    def summed(index):
        return jnp.sum(mom[index].T, axis=0, keepdims=True)

    mom_all[my_row] = jnp.concatenate([summed(0), summed(1), jnp.zeros((6, LANES), F32)], axis=0)
    mom_copies = []
    for k in range(1, m):
        copy = remote(mom_all.at[my_row], mom_all.at[my_row], mom_sems, (k,), (me, lax.rem(my_row + k, m)))
        copy.start()
        mom_copies.append(copy)

    phase_copies = start_pair(phase.at[0], phase.at[rows - 1], halo.at[0], halo_sems.at[0])
    coher_copies = start_pair(coher.at[0], coher.at[rows - 1], halo.at[1], halo_sems.at[1])
    for q in range(1, half - 1):
        smooth_rows(2 * q + 1, 2 * q + 3)
        w_copies.append(exchange(w_send, w_all, w_sems, q, 2 * q + 1, 2 * q + 3))

    date = lax.broadcasted_iota(jnp.int32, (KPAD, ifgs), 0)
    date = jnp.where(date >= DPAD, date - DPAD, date)
    signs = (date == pairs[1:2, :]).astype(F32) - (date == pairs[0:1, :]).astype(F32)
    gt[:, :ifgs] = signs[:DPAD].astype(BF16)
    gt[:, ifgs:] = signs[:DPAD].astype(BF16)
    g[...] = signs.T.astype(BF16)

    pixel = lax.broadcasted_iota(jnp.int32, (rows * LANES, 2 * LANES), 0)
    slot = lax.broadcasted_iota(jnp.int32, (rows * LANES, 2 * LANES), 1)
    first_pixel = jnp.where(slot < rows, slot * LANES, -1)
    last_pixel = jnp.where((slot >= LANES) & (slot < LANES + rows), (slot - LANES) * LANES + LANES - 1, -1)
    pick[...] = ((pixel == first_pixel) | (pixel == last_pixel)).astype(F32).astype(BF16)
    slot = lax.broadcasted_iota(jnp.int32, (2 * LANES, rows * LANES), 0)
    pixel = lax.broadcasted_iota(jnp.int32, (2 * LANES, rows * LANES), 1)
    first_pixel = jnp.where(slot < rows, slot * LANES, -1)
    last_pixel = jnp.where((slot >= LANES) & (slot < LANES + rows), (slot - LANES) * LANES + LANES - 1, -1)
    place[...] = ((pixel == first_pixel) | (pixel == last_pixel)).astype(F32).astype(BF16)

    for copy in mom_copies:
        copy.wait()
    sums = mom_all[0]
    for k in range(1, m):
        sums = sums + mom_all[k]
    slope = sums[0:1, :] / sums[1:2, :]
    topo_out[...] = slope[:, :count]
    topo_s[...] = jnp.broadcast_to(slope, (LANES, LANES)).T

    def correct_rows(low, high):
        def body(c, _):
            i0 = pl.multiple_of(c * CHUNK, CHUNK)
            column = topo_s[pl.ds(i0, CHUNK), :]
            for j in range(low, high):
                for d in range(n):
                    cols = pl.ds(d * LANES, LANES)
                    value = sm_s[j, pl.ds(i0, CHUNK), cols] - column * height[j:j + 1, cols]
                    c_send[d, j, pl.ds(i0, CHUNK), :] = value.astype(BF16)
            return 0

        lax.fori_loop(0, chunks, body, 0)

    c_copies = []
    for q in range(half - 1):
        correct_rows(2 * q + 1, 2 * q + 3)
        c_copies.append(exchange(c_send, c_all, c_sems, q, 2 * q + 1, 2 * q + 3))
    wait_pair(phase_copies, halo.at[0])
    wait_pair(coher_copies, halo.at[1])
    last = []
    for part, j in ((half - 1, rows - 1), (half, 0)):
        smooth_rows(j, j + 1)
        last += exchange(w_send, w_all, w_sems, part, j, j + 1)
        correct_rows(j, j + 1)
        last += exchange(c_send, c_all, c_sems, part, j, j + 1)

    def pair(q):
        return 2 * q + 1, (2 * q + 2) % rows

    def both(q, of):
        return jnp.concatenate([of(j) for j in pair(q)], axis=1)

    def put(target, q, value):
        for i, j in enumerate(pair(q)):
            target[j] = value[:, i * LANES:(i + 1) * LANES]

    def back_project(u):
        return dot(gt[...], jnp.concatenate(split(u), axis=0))

    def right_rows(q):
        put(r_s, q, back_project(both(q, lambda j: w_all[j].astype(F32) * c_all[j].astype(F32))))

    def weighted(v, target, q):
        high, low = split(both(q, lambda j: v[j]))
        filler = jnp.zeros((KPAD - 2 * DPAD, 2 * LANES), BF16)
        diff = dot(g[...], jnp.concatenate([high, low, filler], axis=0))
        put(target, q, back_project(diff * both(q, lambda j: w_all[j].astype(F32))))

    small = lax.broadcasted_iota(jnp.int32, (DPAD, LANES), 1)

    def start_halo(v, step):
        pack[step, 0] = v[0].astype(BF16)
        pack[step, 1] = v[rows - 1].astype(BF16)
        packed = dot(jnp.concatenate([v[j].astype(BF16) for j in range(rows)], axis=1), pick[...])
        pack[step, 2] = packed[:, :LANES].astype(BF16)
        pack[step, 3] = packed[:, LANES:].astype(BF16)
        left, right = (lax.max(me - 1, 0), my_row), (lax.min(me + 1, n - 1), my_row)
        copies = (
            (has_up, remote(pack.at[step, 0], halo_row.at[step, 1], row_sems, (step, 0), up)),
            (has_down, remote(pack.at[step, 1], halo_row.at[step, 0], row_sems, (step, 1), down)),
            (has_left, remote(pack.at[step, 2], halo_col.at[step, 1], col_sems, (step, 0), left)),
            (has_right, remote(pack.at[step, 3], halo_col.at[step, 0], col_sems, (step, 1), right)),
        )
        for there, copy in copies:
            pl.when(there)(copy.start)
        return copies

    def wait_halo(copies, step):
        for there, copy in copies:
            pl.when(there)(copy.wait_send)
        for index, buffer in ((0, halo_row), (1, halo_col)):
            low_there, low_copy = copies[2 * index]
            high_there, high_copy = copies[2 * index + 1]
            for side, there, copy in ((0, low_there, high_copy), (1, high_there, low_copy)):
                pl.when(there)(copy.wait_recv)

                @pl.when(jnp.logical_not(there))
                def _(side=side, buffer=buffer):
                    buffer[step, side] = jnp.zeros((DPAD, LANES), BF16)

    def spread_and_halo(v, target, step, copies):
        for j in range(rows):
            here = v[j]
            around = jnp.where(small == 0, 0.0, pltpu.roll(here, 1, 1))
            around += jnp.where(small == LANES - 1, 0.0, pltpu.roll(here, LANES - 1, 1))
            if j:
                around += v[j - 1]
            if j < rows - 1:
                around += v[j + 1]
            spread = 4.0 * here - around
            target[j] = target[j] + SMOOTHING_WEIGHT * spread + RIDGE_WEIGHT * here
        wait_halo(copies, step)
        beside = dot(jnp.concatenate([halo_col[step, 0], halo_col[step, 1]], axis=1), place[...])
        for j in range(rows):
            around = beside[:, j * LANES:(j + 1) * LANES]
            if j == 0:
                around = around + halo_row[step, 0].astype(F32)
            if j == rows - 1:
                around = around + halo_row[step, 1].astype(F32)
            target[j] = target[j] - SMOOTHING_WEIGHT * around

    def apply(v, target, step, middle):
        copies = start_halo(v, step)
        for q in range(half):
            weighted(v, target, q)
            if q == half // 2 - 1:
                middle()
        spread_and_halo(v, target, step, copies)

    def fold(value):
        return jnp.sum(value, axis=0, keepdims=True)

    def reduce_first(step, parts):
        filled = list(parts) + [jnp.zeros((8 - len(parts), LANES), F32)]
        red_a[step, me] = jnp.concatenate(filled, axis=0)
        copies = []
        for k in range(1, n):
            copy = remote(red_a.at[step, me], red_a.at[step, me], a_sems, (step, k), (lax.rem(me + k, n), my_row))
            copy.start()
            copies.append(copy)
        return copies

    def reduce_second(step, copies):
        for copy in copies:
            copy.wait()
        total = red_a[step, 0]
        for k in range(1, n):
            total = total + red_a[step, k]
        red_b[step, my_row] = total
        later = []
        for k in range(1, m):
            copy = remote(red_b.at[step, my_row], red_b.at[step, my_row], b_sems, (step, k), (me, lax.rem(my_row + k, m)))
            copy.start()
            later.append(copy)
        return later

    def reduce_last(step, copies):
        for copy in copies:
            copy.wait()
        total = red_b[step, 0]
        for k in range(1, m):
            total = total + red_b[step, k]
        total = jnp.sum(total, axis=1, keepdims=True)
        return [total[i:i + 1, :] for i in range(3)]

    def overlapped(step, parts, v, target, apply_step):
        state = {"copies": reduce_first(step, parts)}

        def middle():
            state["copies"] = reduce_second(step, state["copies"])

        apply(v, target, apply_step, middle)
        return reduce_last(step, state["copies"])

    for q in range(half - 1):
        for copy in w_copies[q] + c_copies[q]:
            copy.wait()
        right_rows(q)
        weighted(r_s, w_s, q)
    for copy in last:
        copy.wait()
    right_rows(half - 1)
    copies = start_halo(r_s, 0)
    weighted(r_s, w_s, half - 1)
    spread_and_halo(r_s, w_s, 0, copies)
    gamma_sum = jnp.zeros((1, LANES), F32)
    delta_sum = jnp.zeros((1, LANES), F32)
    for j in range(rows):
        gamma_sum += fold(r_s[j] * r_s[j])
        delta_sum += fold(r_s[j] * w_s[j])
    gamma, curve, _ = overlapped(0, (gamma_sum, delta_sum), w_s, n_s, 1)

    alpha = gamma / curve
    alpha_first = alpha
    gamma_sum = jnp.zeros((1, LANES), F32)
    delta_sum = jnp.zeros((1, LANES), F32)
    cross_sum = jnp.zeros((1, LANES), F32)
    for j in range(rows):
        p, s, z = r_s[j], w_s[j], n_s[j]
        r = p - alpha * s
        w = s - alpha * z
        p_s[j], s_s[j], z_s[j] = p, s, z
        r_s[j], w_s[j] = r, w
        gamma_sum += fold(r * r)
        delta_sum += fold(r * w)
        cross_sum += fold(r * s)
    gamma_next, delta, cross = overlapped(1, (gamma_sum, delta_sum, cross_sum), w_s, n_s, 2)

    beta = gamma_next / gamma
    gamma = gamma_next
    curve = delta + 2.0 * beta * cross + beta * beta * curve
    alpha = gamma / curve
    gamma_sum = jnp.zeros((1, LANES), F32)
    delta_sum = jnp.zeros((1, LANES), F32)
    cross_sum = jnp.zeros((1, LANES), F32)
    for j in range(rows):
        r, w = r_s[j], w_s[j]
        first_p = p_s[j]
        p = r + beta * first_p
        s = w + beta * s_s[j]
        z = n_s[j] + beta * z_s[j]
        r = r - alpha * s
        w = w - alpha * z
        p_s[j] = p
        r_s[j] = r
        z_s[j] = alpha_first * first_p + alpha * p
        gamma_sum += fold(r * r)
        delta_sum += fold(r * w)
        cross_sum += fold(r * s)
    copies = reduce_first(2, (gamma_sum, delta_sum, cross_sum))
    gamma_next, delta, cross = reduce_last(2, reduce_second(2, copies))
    beta = gamma_next / gamma
    curve = delta + 2.0 * beta * cross + beta * beta * curve
    alpha = gamma_next / curve
    for j in range(rows):
        x_out[j] = z_s[j] + alpha * (r_s[j] + beta * p_s[j])


def order_dates(x, topo, out, topo_out):
    out[...] = jnp.swapaxes(x[...], 0, 1)
    topo_out[...] = topo[...]


def solution(mesh):
    n, m = mesh.shape["ifg"], mesh.shape["rows"]

    def per_device(phase, coherence, height, gap_mask, date_pairs):
        count, rows, width = phase.shape
        ifgs = date_pairs.shape[0]
        dma = pltpu.SemaphoreType.DMA
        state = pltpu.VMEM((rows, DPAD, LANES), F32)
        vmem = pl.BlockSpec(memory_space=pltpu.VMEM)
        field, topo = pl.pallas_call(
            functools.partial(kernel, n, m),
            out_shape=(
                jax.ShapeDtypeStruct((rows, DPAD, LANES), F32),
                jax.ShapeDtypeStruct((1, count), F32),
            ),
            in_specs=[vmem] * 5,
            out_specs=(vmem, vmem),
            scratch_shapes=[
                pltpu.VMEM((2, 2, count, width), BF16),
                pltpu.VMEM((rows, count, width), F32),
                pltpu.VMEM((n, rows, count, LANES), BF16),
                pltpu.VMEM((rows, ifgs, LANES), BF16),
                pltpu.VMEM((n, rows, count, LANES), BF16),
                pltpu.VMEM((rows, ifgs, LANES), BF16),
                pltpu.VMEM((2, rows, width), F32),
                pltpu.VMEM((count, rows), F32),
                pltpu.VMEM((2, LANES, LANES), F32),
                pltpu.VMEM((m, 8, LANES), F32),
                pltpu.VMEM((LANES, LANES), F32),
                pltpu.VMEM((ifgs, KPAD), BF16),
                pltpu.VMEM((DPAD, 2 * ifgs), BF16),
                pltpu.VMEM((rows * LANES, 2 * LANES), BF16),
                pltpu.VMEM((2 * LANES, rows * LANES), BF16),
                state, state, state, state, state, state,
                pltpu.VMEM((3, 4, DPAD, LANES), BF16),
                pltpu.VMEM((3, 2, DPAD, LANES), BF16),
                pltpu.VMEM((3, 2, DPAD, LANES), BF16),
                pltpu.VMEM((3, n, 8, LANES), F32),
                pltpu.VMEM((3, m, 8, LANES), F32),
                dma((2, 2)),
                dma((2, 2, 2)),
                dma((2, rows // 2 + 1, n)),
                dma((2, rows // 2 + 1, n)),
                dma((2, m)),
                dma((2, 3, 2)),
                dma((2, 3, 2)),
                dma((2, 3, n)),
                dma((2, 3, m)),
            ],
            compiler_params=pltpu.CompilerParams(
                collective_id=0, has_side_effects=True, vmem_limit_bytes=56 * 1024 * 1024
            ),
        )(phase.transpose(1, 0, 2), coherence.transpose(1, 0, 2), height, gap_mask.T, date_pairs.T)
        displacement, topo = pl.pallas_call(
            order_dates,
            grid=(pl.cdiv(DATES, BLOCK),),
            out_shape=(
                jax.ShapeDtypeStruct((DATES, rows, LANES), F32),
                jax.ShapeDtypeStruct((1, count), F32),
            ),
            in_specs=[
                pl.BlockSpec((rows, BLOCK, LANES), lambda i: (0, i, 0)),
                pl.BlockSpec((1, count), lambda i: (0, 0)),
            ],
            out_specs=(
                pl.BlockSpec((BLOCK, rows, LANES), lambda i: (i, 0, 0)),
                pl.BlockSpec((1, count), lambda i: (0, 0)),
            ),
        )(field, topo)
        return displacement, topo.reshape(count)

    return jax.shard_map(
        per_device,
        mesh=mesh,
        in_specs=(
            P("ifg", "rows", None),
            P("ifg", "rows", None),
            P("rows", None),
            P("ifg", "rows"),
            P(),
        ),
        out_specs=(P(None, "rows", "ifg"), P("ifg")),
        check_vma=False,
    )
```

```python
import functools

import jax
import jax.numpy as jnp
from jax import lax
from jax.experimental import pallas as pl
from jax.experimental.pallas import tpu as pltpu
from jax.sharding import PartitionSpec as P

DATES = 300
DPAD = 304
KPAD = 640
LANES = 128
CHUNK = 16
BLOCK = 104
SMOOTHING_WEIGHT = 0.5
RIDGE_WEIGHT = 0.05
F32 = jnp.float32
BF16 = jnp.bfloat16
MESH = pl.DeviceIdType.MESH


def split(value):
    high = value.astype(BF16)
    low = (value - high.astype(F32)).astype(BF16)
    return high, low


def dot(a, b):
    return jnp.dot(a, b, preferred_element_type=F32)


def kernel(
    n, m,
    phase, coher, height, gap, pairs,
    x_out, topo_out,
    ph_s, co_s, edge, halo, sm_s, w_send, w_all, c_send, c_all,
    h_halo, gap_s, mom, mom_all, topo_s, g, gt, pick, place,
    r_s, w_s, n_s, p_s, s_s, z_s,
    pack, halo_row, halo_col, red_a, red_b,
    h_sems, halo_sems, w_sems, c_sems, mom_sems, row_sems, col_sems, a_sems, b_sems,
):
    count, rows, width = phase.shape
    ifgs = pairs.shape[1]
    tiles = width // LANES
    chunks = count // CHUNK
    me = lax.axis_index("ifg")
    my_row = lax.axis_index("rows")
    has_up, has_down = my_row > 0, my_row < m - 1
    has_left, has_right = me > 0, me < n - 1

    barrier = pltpu.get_barrier_semaphore()
    for k in range(1, n):
        pl.semaphore_signal(barrier, inc=1, device_id=(lax.rem(me + k, n), my_row), device_id_type=MESH)
    for k in range(1, m):
        pl.semaphore_signal(barrier, inc=1, device_id=(me, lax.rem(my_row + k, m)), device_id_type=MESH)

    def remote(src, dst, sems, index, target):
        return pltpu.make_async_remote_copy(
            src_ref=src, dst_ref=dst,
            send_sem=sems.at[(0,) + index], recv_sem=sems.at[(1,) + index],
            device_id=target, device_id_type=MESH,
        )

    def widen(c, _):
        for src, dst in ((phase, ph_s), (coher, co_s)):
            block = src[pl.ds(c * CHUNK, CHUNK)].astype(F32).reshape(CHUNK * rows, width)
            for t in range(tiles):
                dst[t, pl.ds(pl.multiple_of(c * CHUNK * rows, CHUNK * rows), CHUNK * rows), :] = (
                    block[:, t * LANES:(t + 1) * LANES]
                )
        return 0

    lax.fori_loop(0, chunks, widen, 0)

    def row_of(ref, j, i0, size):
        return jnp.concatenate(
            [ref[t, pl.ds(i0 * rows + j, size, stride=rows), :] for t in range(tiles)], axis=1
        )

    gap_s[...] = gap[...].astype(F32).T
    pl.semaphore_wait(barrier, n + m - 2)
    up, down = (me, lax.max(my_row - 1, 0)), (me, lax.min(my_row + 1, m - 1))

    def start_pair(sent_up, sent_down, landing, sems):
        to_up = remote(sent_up, landing.at[1], sems, (0,), up)
        to_down = remote(sent_down, landing.at[0], sems, (1,), down)
        pl.when(has_up)(to_up.start)
        pl.when(has_down)(to_down.start)
        return to_up, to_down

    def wait_pair(copies, landing):
        to_up, to_down = copies
        for there, sent, received, side in ((has_up, to_up, to_down, 0), (has_down, to_down, to_up, 1)):
            pl.when(there)(sent.wait_send)
            pl.when(there)(received.wait_recv)

            @pl.when(jnp.logical_not(there))
            def _(side=side):
                landing[side] = jnp.zeros_like(landing[side])

    terrain_copies = start_pair(height, height, h_halo, h_sems)

    def take_edges(c, _):
        i0 = pl.multiple_of(c * CHUNK, CHUNK)
        for side, j in ((0, 0), (1, rows - 1)):
            for a, ref in ((0, ph_s), (1, co_s)):
                edge[side, a, pl.ds(i0, CHUNK), :] = row_of(ref, j, i0, CHUNK).astype(BF16)
        return 0


    def box(vert):
        lane = lax.broadcasted_iota(jnp.int32, vert.shape, 1)
        before = jnp.where(lane == 0, 0.0, pltpu.roll(vert, 1, 1))
        after = jnp.where(lane == width - 1, 0.0, pltpu.roll(vert, width - 1, 1))
        return vert + before + after

    def smooth_rows(low, high):
        def body(c, _):
            i0 = pl.multiple_of(c * CHUNK, CHUNK)
            gaps = gap_s[pl.ds(i0, CHUNK), :]

            def load(j):
                if j < 0 or j == rows:
                    side = 0 if j < 0 else 1
                    ph = halo[side, 0, pl.ds(i0, CHUNK), :].astype(F32)
                    co = halo[side, 1, pl.ds(i0, CHUNK), :].astype(F32)
                else:
                    ph = row_of(ph_s, j, i0, CHUNK)
                    co = row_of(co_s, j, i0, CHUNK)
                return ph * co, co

            window = [load(low - 1), load(low)]
            for j in range(low, high):
                window.append(load(j + 1))
                numer = box(window[0][0] + window[1][0] + window[2][0])
                denom = box(window[0][1] + window[1][1] + window[2][1])
                window.pop(0)
                smooth = numer / denom
                mean = denom * (1.0 / 9.0)
                weight = (gaps[:, j:j + 1] * mean).astype(BF16)
                for d in range(n):
                    w_send[d, j, pl.ds(i0, CHUNK), :] = weight[:, d * LANES:(d + 1) * LANES]
                sm_s[j, pl.ds(i0, CHUNK), :] = smooth
            return 0

        lax.fori_loop(0, chunks, body, 0)

    mine = pl.ds(pl.multiple_of(me * count, count), count)

    def exchange(src, dst, sems, part, low, high):
        span = pl.ds(low, high - low)
        copies = []
        for k in range(n - 1, 0, -1):
            d = lax.rem(me + k, n)
            copy = remote(src.at[d, span], dst.at[span, mine, :], sems, (part, k), (d, my_row))
            copy.start()
            copies.append(copy)
        own = pltpu.make_async_copy(src.at[me, span], dst.at[span, mine, :], sems.at[0, part, 0])
        own.start()
        copies.append(own)
        return copies

    half = rows // 2
    smooth_rows(1, 3)
    w_copies = [exchange(w_send, w_all, w_sems, 0, 1, 3)]

    wait_pair(terrain_copies, h_halo)

    def box_terrain(take):
        here = take(height[...])
        above = take(h_halo[0])[rows - 1:]
        below = take(h_halo[1])[:1]
        vert = here + jnp.concatenate([above, here[:-1]], axis=0) + jnp.concatenate([here[1:], below], axis=0)
        return box(vert)

    terrain_box = box_terrain(lambda h: h)
    square_box = box_terrain(lambda h: h * h)

    def moments(c, _):
        start = pl.multiple_of(c * CHUNK * rows, CHUNK * rows)
        top = jnp.zeros((CHUNK, rows, LANES), F32)
        low = jnp.zeros((CHUNK, rows, LANES), F32)
        for t in range(tiles):
            cols = slice(t * LANES, (t + 1) * LANES)
            co = co_s[t, pl.ds(start, CHUNK * rows), :].reshape(CHUNK, rows, LANES)
            ph = ph_s[t, pl.ds(start, CHUNK * rows), :].reshape(CHUNK, rows, LANES)
            top += co * ph * terrain_box[None, :, cols]
            low += co * square_box[None, :, cols]
        mom[0, pl.ds(start, CHUNK * rows), :] = top.reshape(CHUNK * rows, LANES)
        mom[1, pl.ds(start, CHUNK * rows), :] = low.reshape(CHUNK * rows, LANES)
        return 0

    lax.fori_loop(0, chunks, moments, 0)

    def summed(index):
        total = mom[index, pl.ds(0, count, stride=rows), :]
        for j in range(1, rows):
            total += mom[index, pl.ds(j, count, stride=rows), :]
        if count < LANES:
            total = jnp.concatenate([total, jnp.zeros((LANES - count, LANES), F32)], axis=0)
        return jnp.sum(total.T, axis=0, keepdims=True)

    mom_all[my_row] = jnp.concatenate([summed(0), summed(1), jnp.zeros((6, LANES), F32)], axis=0)
    mom_copies = []
    for k in range(1, m):
        copy = remote(mom_all.at[my_row], mom_all.at[my_row], mom_sems, (k,), (me, lax.rem(my_row + k, m)))
        copy.start()
        mom_copies.append(copy)

    lax.fori_loop(0, chunks, take_edges, 0)
    edge_copies = start_pair(edge.at[0], edge.at[1], halo, halo_sems)
    for q in range(1, half - 1):
        smooth_rows(2 * q + 1, 2 * q + 3)
        w_copies.append(exchange(w_send, w_all, w_sems, q, 2 * q + 1, 2 * q + 3))

    date = lax.broadcasted_iota(jnp.int32, (KPAD, ifgs), 0)
    date = jnp.where(date >= DPAD, date - DPAD, date)
    signs = (date == pairs[1:2, :]).astype(F32) - (date == pairs[0:1, :]).astype(F32)
    gt[:, :ifgs] = signs[:DPAD].astype(BF16)
    gt[:, ifgs:] = signs[:DPAD].astype(BF16)
    g[...] = signs.T.astype(BF16)

    pixel = lax.broadcasted_iota(jnp.int32, (rows * LANES, 2 * LANES), 0)
    slot = lax.broadcasted_iota(jnp.int32, (rows * LANES, 2 * LANES), 1)
    first_pixel = jnp.where(slot < rows, slot * LANES, -1)
    last_pixel = jnp.where((slot >= LANES) & (slot < LANES + rows), (slot - LANES) * LANES + LANES - 1, -1)
    pick[...] = ((pixel == first_pixel) | (pixel == last_pixel)).astype(F32).astype(BF16)
    slot = lax.broadcasted_iota(jnp.int32, (2 * LANES, rows * LANES), 0)
    pixel = lax.broadcasted_iota(jnp.int32, (2 * LANES, rows * LANES), 1)
    first_pixel = jnp.where(slot < rows, slot * LANES, -1)
    last_pixel = jnp.where((slot >= LANES) & (slot < LANES + rows), (slot - LANES) * LANES + LANES - 1, -1)
    place[...] = ((pixel == first_pixel) | (pixel == last_pixel)).astype(F32).astype(BF16)

    for copy in mom_copies:
        copy.wait()
    sums = mom_all[0]
    for k in range(1, m):
        sums = sums + mom_all[k]
    slope = sums[0:1, :] / sums[1:2, :]
    topo_out[...] = slope[:, :count]
    topo_s[...] = jnp.broadcast_to(slope, (LANES, LANES)).T

    def correct_rows(low, high):
        def body(c, _):
            i0 = pl.multiple_of(c * CHUNK, CHUNK)
            column = topo_s[pl.ds(i0, CHUNK), :]
            for j in range(low, high):
                for d in range(n):
                    cols = pl.ds(d * LANES, LANES)
                    value = sm_s[j, pl.ds(i0, CHUNK), cols] - column * height[j:j + 1, cols]
                    c_send[d, j, pl.ds(i0, CHUNK), :] = value.astype(BF16)
            return 0

        lax.fori_loop(0, chunks, body, 0)

    c_copies = []
    for q in range(half - 1):
        correct_rows(2 * q + 1, 2 * q + 3)
        c_copies.append(exchange(c_send, c_all, c_sems, q, 2 * q + 1, 2 * q + 3))
    wait_pair(edge_copies, halo)
    last = []
    for part, j in ((half - 1, rows - 1), (half, 0)):
        smooth_rows(j, j + 1)
        last += exchange(w_send, w_all, w_sems, part, j, j + 1)
        correct_rows(j, j + 1)
        last += exchange(c_send, c_all, c_sems, part, j, j + 1)

    def pair(q):
        return 2 * q + 1, (2 * q + 2) % rows

    def both(q, of):
        return jnp.concatenate([of(j) for j in pair(q)], axis=1)

    def put(target, q, value):
        for i, j in enumerate(pair(q)):
            target[j] = value[:, i * LANES:(i + 1) * LANES]

    def back_project(u):
        return dot(gt[...], jnp.concatenate(split(u), axis=0))

    def right_rows(q):
        put(r_s, q, back_project(both(q, lambda j: w_all[j].astype(F32) * c_all[j].astype(F32))))

    def weighted(v, target, q):
        high, low = split(both(q, lambda j: v[j]))
        filler = jnp.zeros((KPAD - 2 * DPAD, 2 * LANES), BF16)
        diff = dot(g[...], jnp.concatenate([high, low, filler], axis=0))
        put(target, q, back_project(diff * both(q, lambda j: w_all[j].astype(F32))))

    small = lax.broadcasted_iota(jnp.int32, (DPAD, LANES), 1)

    def start_halo(v, step):
        left, right = (lax.max(me - 1, 0), my_row), (lax.min(me + 1, n - 1), my_row)
        copies = (
            (has_up, remote(pack.at[step, 0], halo_row.at[step, 1], row_sems, (step, 0), up)),
            (has_down, remote(pack.at[step, 1], halo_row.at[step, 0], row_sems, (step, 1), down)),
            (has_left, remote(pack.at[step, 2], halo_col.at[step, 1], col_sems, (step, 0), left)),
            (has_right, remote(pack.at[step, 3], halo_col.at[step, 0], col_sems, (step, 1), right)),
        )
        pack[step, 0] = v[0].astype(BF16)
        pack[step, 1] = v[rows - 1].astype(BF16)
        for there, copy in copies[:2]:
            pl.when(there)(copy.start)
        packed = dot(jnp.concatenate([v[j].astype(BF16) for j in range(rows)], axis=1), pick[...])
        pack[step, 2] = packed[:, :LANES].astype(BF16)
        pack[step, 3] = packed[:, LANES:].astype(BF16)
        for there, copy in copies[2:]:
            pl.when(there)(copy.start)
        return copies

    def wait_halo(copies, step):
        for there, copy in copies:
            pl.when(there)(copy.wait_send)
        for index, buffer in ((0, halo_row), (1, halo_col)):
            low_there, low_copy = copies[2 * index]
            high_there, high_copy = copies[2 * index + 1]
            for side, there, copy in ((0, low_there, high_copy), (1, high_there, low_copy)):
                pl.when(there)(copy.wait_recv)

                @pl.when(jnp.logical_not(there))
                def _(side=side, buffer=buffer):
                    buffer[step, side] = jnp.zeros((DPAD, LANES), BF16)

    def spread_and_halo(v, target, step, copies):
        for j in range(rows):
            here = v[j]
            around = jnp.where(small == 0, 0.0, pltpu.roll(here, 1, 1))
            around += jnp.where(small == LANES - 1, 0.0, pltpu.roll(here, LANES - 1, 1))
            if j:
                around += v[j - 1]
            if j < rows - 1:
                around += v[j + 1]
            spread = 4.0 * here - around
            target[j] = target[j] + SMOOTHING_WEIGHT * spread + RIDGE_WEIGHT * here
        wait_halo(copies, step)
        beside = dot(jnp.concatenate([halo_col[step, 0], halo_col[step, 1]], axis=1), place[...])
        for j in range(rows):
            around = beside[:, j * LANES:(j + 1) * LANES]
            if j == 0:
                around = around + halo_row[step, 0].astype(F32)
            if j == rows - 1:
                around = around + halo_row[step, 1].astype(F32)
            target[j] = target[j] - SMOOTHING_WEIGHT * around

    def apply(v, target, step, middle):
        copies = start_halo(v, step)
        for q in range(half):
            weighted(v, target, q)
            if q == half // 2 - 1:
                middle()
        spread_and_halo(v, target, step, copies)

    def fold(value):
        return jnp.sum(value, axis=0, keepdims=True)

    def reduce_first(step, parts):
        filled = list(parts) + [jnp.zeros((8 - len(parts), LANES), F32)]
        red_b[step, my_row] = jnp.concatenate(filled, axis=0)
        copies = []
        for k in range(1, m):
            copy = remote(red_b.at[step, my_row], red_b.at[step, my_row], b_sems, (step, k), (me, lax.rem(my_row + k, m)))
            copy.start()
            copies.append(copy)
        return copies

    def reduce_second(step, copies):
        for copy in copies:
            copy.wait()
        total = red_b[step, 0]
        for k in range(1, m):
            total = total + red_b[step, k]
        red_a[step, me] = total
        later = []
        for k in range(1, n):
            copy = remote(red_a.at[step, me], red_a.at[step, me], a_sems, (step, k), (lax.rem(me + k, n), my_row))
            copy.start()
            later.append(copy)
        return later

    def reduce_last(step, copies):
        for copy in copies:
            copy.wait()
        total = red_a[step, 0]
        for k in range(1, n):
            total = total + red_a[step, k]
        total = jnp.sum(total, axis=1, keepdims=True)
        return [total[i:i + 1, :] for i in range(3)]

    def overlapped(step, parts, v, target, apply_step):
        state = {"copies": reduce_first(step, parts)}

        def middle():
            state["copies"] = reduce_second(step, state["copies"])

        apply(v, target, apply_step, middle)
        return reduce_last(step, state["copies"])

    for q in range(half - 1):
        for copy in w_copies[q] + c_copies[q]:
            copy.wait()
        right_rows(q)
        weighted(r_s, w_s, q)
    for copy in last:
        copy.wait()
    right_rows(half - 1)
    copies = start_halo(r_s, 0)
    weighted(r_s, w_s, half - 1)
    spread_and_halo(r_s, w_s, 0, copies)
    gamma_sum = jnp.zeros((1, LANES), F32)
    delta_sum = jnp.zeros((1, LANES), F32)
    for j in range(rows):
        gamma_sum += fold(r_s[j] * r_s[j])
        delta_sum += fold(r_s[j] * w_s[j])
    gamma, curve, _ = overlapped(0, (gamma_sum, delta_sum), w_s, n_s, 1)

    alpha = gamma / curve
    alpha_first = alpha
    gamma_sum = jnp.zeros((1, LANES), F32)
    delta_sum = jnp.zeros((1, LANES), F32)
    cross_sum = jnp.zeros((1, LANES), F32)
    for j in range(rows):
        p, s, z = r_s[j], w_s[j], n_s[j]
        r = p - alpha * s
        w = s - alpha * z
        p_s[j], s_s[j], z_s[j] = p, s, z
        r_s[j], w_s[j] = r, w
        gamma_sum += fold(r * r)
        delta_sum += fold(r * w)
        cross_sum += fold(r * s)
    gamma_next, delta, cross = overlapped(1, (gamma_sum, delta_sum, cross_sum), w_s, n_s, 2)

    beta = gamma_next / gamma
    gamma = gamma_next
    curve = delta + 2.0 * beta * cross + beta * beta * curve
    alpha = gamma / curve
    gamma_sum = jnp.zeros((1, LANES), F32)
    delta_sum = jnp.zeros((1, LANES), F32)
    cross_sum = jnp.zeros((1, LANES), F32)
    for j in range(rows):
        r, w = r_s[j], w_s[j]
        first_p = p_s[j]
        p = r + beta * first_p
        s = w + beta * s_s[j]
        z = n_s[j] + beta * z_s[j]
        r = r - alpha * s
        w = w - alpha * z
        p_s[j] = p
        r_s[j] = r
        z_s[j] = alpha_first * first_p + alpha * p
        gamma_sum += fold(r * r)
        delta_sum += fold(r * w)
        cross_sum += fold(r * s)
    copies = reduce_first(2, (gamma_sum, delta_sum, cross_sum))
    gamma_next, delta, cross = reduce_last(2, reduce_second(2, copies))
    beta = gamma_next / gamma
    curve = delta + 2.0 * beta * cross + beta * beta * curve
    alpha = gamma_next / curve
    for j in range(rows):
        x_out[j] = z_s[j] + alpha * (r_s[j] + beta * p_s[j])


def order_dates(x, topo, out, topo_out):
    rows, dates, _ = x.shape
    for j in range(rows):
        out[pl.ds(j, dates, stride=rows), :] = x[j]
    topo_out[...] = topo[...]


def solution(mesh):
    n, m = mesh.shape["ifg"], mesh.shape["rows"]

    def per_device(phase, coherence, height, gap_mask, date_pairs):
        count, rows, width = phase.shape
        ifgs = date_pairs.shape[0]
        tiles = width // LANES
        dma = pltpu.SemaphoreType.DMA
        state = pltpu.VMEM((rows, DPAD, LANES), F32)
        vmem = pl.BlockSpec(memory_space=pltpu.VMEM)
        field, topo = pl.pallas_call(
            functools.partial(kernel, n, m),
            out_shape=(
                jax.ShapeDtypeStruct((rows, DPAD, LANES), F32),
                jax.ShapeDtypeStruct((1, count), F32),
            ),
            in_specs=[vmem] * 5,
            out_specs=(vmem, vmem),
            scratch_shapes=[
                pltpu.VMEM((tiles, count * rows, LANES), F32),
                pltpu.VMEM((tiles, count * rows, LANES), F32),
                pltpu.VMEM((2, 2, count, width), BF16),
                pltpu.VMEM((2, 2, count, width), BF16),
                pltpu.VMEM((rows, count, width), F32),
                pltpu.VMEM((n, rows, count, LANES), BF16),
                pltpu.VMEM((rows, ifgs, LANES), BF16),
                pltpu.VMEM((n, rows, count, LANES), BF16),
                pltpu.VMEM((rows, ifgs, LANES), BF16),
                pltpu.VMEM((2, rows, width), F32),
                pltpu.VMEM((count, rows), F32),
                pltpu.VMEM((2, count * rows, LANES), F32),
                pltpu.VMEM((m, 8, LANES), F32),
                pltpu.VMEM((LANES, LANES), F32),
                pltpu.VMEM((ifgs, KPAD), BF16),
                pltpu.VMEM((DPAD, 2 * ifgs), BF16),
                pltpu.VMEM((rows * LANES, 2 * LANES), BF16),
                pltpu.VMEM((2 * LANES, rows * LANES), BF16),
                state, state, state, state, state, state,
                pltpu.VMEM((3, 4, DPAD, LANES), BF16),
                pltpu.VMEM((3, 2, DPAD, LANES), BF16),
                pltpu.VMEM((3, 2, DPAD, LANES), BF16),
                pltpu.VMEM((3, n, 8, LANES), F32),
                pltpu.VMEM((3, m, 8, LANES), F32),
                dma((2, 2)),
                dma((2, 2)),
                dma((2, rows // 2 + 1, n)),
                dma((2, rows // 2 + 1, n)),
                dma((2, m)),
                dma((2, 3, 2)),
                dma((2, 3, 2)),
                dma((2, 3, n)),
                dma((2, 3, m)),
            ],
            compiler_params=pltpu.CompilerParams(
                collective_id=0, has_side_effects=True, vmem_limit_bytes=56 * 1024 * 1024
            ),
        )(phase, coherence, height, gap_mask.T, date_pairs.T)
        displacement, topo = pl.pallas_call(
            order_dates,
            grid=(pl.cdiv(DATES, BLOCK),),
            out_shape=(
                jax.ShapeDtypeStruct((DATES * rows, LANES), F32),
                jax.ShapeDtypeStruct((1, count), F32),
            ),
            in_specs=[
                pl.BlockSpec((rows, BLOCK, LANES), lambda i: (0, i, 0)),
                pl.BlockSpec((1, count), lambda i: (0, 0)),
            ],
            out_specs=(
                pl.BlockSpec((BLOCK * rows, LANES), lambda i: (i, 0)),
                pl.BlockSpec((1, count), lambda i: (0, 0)),
            ),
        )(field, topo)
        return displacement.reshape(DATES, rows, LANES), topo.reshape(count)

    return jax.shard_map(
        per_device,
        mesh=mesh,
        in_specs=(
            P("ifg", "rows", None),
            P("ifg", "rows", None),
            P("rows", None),
            P("ifg", "rows"),
            P(),
        ),
        out_specs=(P(None, "rows", "ifg"), P("ifg")),
        check_vma=False,
    )
```

```python
import functools

import jax
import jax.numpy as jnp
from jax import lax
from jax.experimental import pallas as pl
from jax.experimental.pallas import tpu as pltpu
from jax.sharding import PartitionSpec as P

DATES = 300
DPAD = 304
KPAD = 640
LANES = 128
CHUNK = 16
BLOCK = 304
SMOOTHING_WEIGHT = 0.5
RIDGE_WEIGHT = 0.05
F32 = jnp.float32
BF16 = jnp.bfloat16
MESH = pl.DeviceIdType.MESH


def split(value):
    high = value.astype(BF16)
    low = (value - high.astype(F32)).astype(BF16)
    return high, low


def dot(a, b):
    return jnp.dot(a, b, preferred_element_type=F32)


def kernel(
    n, m,
    phase, coher, height, gap, pairs,
    x_out, topo_out,
    ph_s, co_s, edge, halo, sm_s, w_send, w_all, c_send, c_all,
    h_halo, gap_s, mom, mom_all, topo_s, g, gt, pick, place,
    r_s, w_s, n_s, p_s, s_s, z_s,
    pack, halo_row, halo_col, red_a, red_b,
    h_sems, halo_sems, w_sems, c_sems, mom_sems, row_sems, col_sems, a_sems, b_sems,
):
    count, rows, width = phase.shape
    ifgs = pairs.shape[1]
    tiles = width // LANES
    chunks = count // CHUNK
    me = lax.axis_index("ifg")
    my_row = lax.axis_index("rows")
    has_up, has_down = my_row > 0, my_row < m - 1
    has_left, has_right = me > 0, me < n - 1

    barrier = pltpu.get_barrier_semaphore()
    for k in range(1, n):
        pl.semaphore_signal(barrier, inc=1, device_id=(lax.rem(me + k, n), my_row), device_id_type=MESH)
    for k in range(1, m):
        pl.semaphore_signal(barrier, inc=1, device_id=(me, lax.rem(my_row + k, m)), device_id_type=MESH)

    def remote(src, dst, sems, index, target):
        return pltpu.make_async_remote_copy(
            src_ref=src, dst_ref=dst,
            send_sem=sems.at[(0,) + index], recv_sem=sems.at[(1,) + index],
            device_id=target, device_id_type=MESH,
        )

    def widen(c, _):
        for src, dst in ((phase, ph_s), (coher, co_s)):
            block = src[pl.ds(c * CHUNK, CHUNK)].astype(F32).reshape(CHUNK * rows, width)
            for t in range(tiles):
                dst[t, pl.ds(pl.multiple_of(c * CHUNK * rows, CHUNK * rows), CHUNK * rows), :] = (
                    block[:, t * LANES:(t + 1) * LANES]
                )
        return 0

    lax.fori_loop(0, chunks, widen, 0)

    def row_of(ref, j, i0, size):
        return jnp.concatenate(
            [ref[t, pl.ds(i0 * rows + j, size, stride=rows), :] for t in range(tiles)], axis=1
        )

    gap_s[...] = gap[...].astype(F32).T
    pl.semaphore_wait(barrier, n + m - 2)
    up, down = (me, lax.max(my_row - 1, 0)), (me, lax.min(my_row + 1, m - 1))

    def start_pair(sent_up, sent_down, landing, sems):
        to_up = remote(sent_up, landing.at[1], sems, (0,), up)
        to_down = remote(sent_down, landing.at[0], sems, (1,), down)
        pl.when(has_up)(to_up.start)
        pl.when(has_down)(to_down.start)
        return to_up, to_down

    def wait_pair(copies, landing):
        to_up, to_down = copies
        for there, sent, received, side in ((has_up, to_up, to_down, 0), (has_down, to_down, to_up, 1)):
            pl.when(there)(sent.wait_send)
            pl.when(there)(received.wait_recv)

            @pl.when(jnp.logical_not(there))
            def _(side=side):
                landing[side] = jnp.zeros_like(landing[side])

    terrain_copies = start_pair(height, height, h_halo, h_sems)

    def take_edges(c, _):
        i0 = pl.multiple_of(c * CHUNK, CHUNK)
        for side, j in ((0, 0), (1, rows - 1)):
            for a, ref in ((0, ph_s), (1, co_s)):
                edge[side, a, pl.ds(i0, CHUNK), :] = row_of(ref, j, i0, CHUNK).astype(BF16)
        return 0


    def box(vert):
        lane = lax.broadcasted_iota(jnp.int32, vert.shape, 1)
        before = jnp.where(lane == 0, 0.0, pltpu.roll(vert, 1, 1))
        after = jnp.where(lane == width - 1, 0.0, pltpu.roll(vert, width - 1, 1))
        return vert + before + after

    def smooth_rows(low, high):
        def body(c, _):
            i0 = pl.multiple_of(c * CHUNK, CHUNK)
            gaps = gap_s[pl.ds(i0, CHUNK), :]

            def load(j):
                if j < 0 or j == rows:
                    side = 0 if j < 0 else 1
                    ph = halo[side, 0, pl.ds(i0, CHUNK), :].astype(F32)
                    co = halo[side, 1, pl.ds(i0, CHUNK), :].astype(F32)
                else:
                    ph = row_of(ph_s, j, i0, CHUNK)
                    co = row_of(co_s, j, i0, CHUNK)
                return ph * co, co

            window = [load(low - 1), load(low)]
            for j in range(low, high):
                window.append(load(j + 1))
                numer = box(window[0][0] + window[1][0] + window[2][0])
                denom = box(window[0][1] + window[1][1] + window[2][1])
                window.pop(0)
                smooth = numer / denom
                mean = denom * (1.0 / 9.0)
                weight = (gaps[:, j:j + 1] * mean).astype(BF16)
                for d in range(n):
                    w_send[d, j, pl.ds(i0, CHUNK), :] = weight[:, d * LANES:(d + 1) * LANES]
                sm_s[j, pl.ds(i0, CHUNK), :] = smooth
            return 0

        lax.fori_loop(0, chunks, body, 0)

    mine = pl.ds(pl.multiple_of(me * count, count), count)

    def exchange(src, dst, sems, part, low, high):
        span = pl.ds(low, high - low)
        copies = []
        for k in range(n - 1, 0, -1):
            d = lax.rem(me + k, n)
            copy = remote(src.at[d, span], dst.at[span, mine, :], sems, (part, k), (d, my_row))
            copy.start()
            copies.append(copy)
        own = pltpu.make_async_copy(src.at[me, span], dst.at[span, mine, :], sems.at[0, part, 0])
        own.start()
        copies.append(own)
        return copies

    half = rows // 2
    smooth_rows(1, 3)
    w_copies = [exchange(w_send, w_all, w_sems, 0, 1, 3)]

    wait_pair(terrain_copies, h_halo)

    def box_terrain(take):
        here = take(height[...])
        above = take(h_halo[0])[rows - 1:]
        below = take(h_halo[1])[:1]
        vert = here + jnp.concatenate([above, here[:-1]], axis=0) + jnp.concatenate([here[1:], below], axis=0)
        return box(vert)

    terrain_box = box_terrain(lambda h: h)
    square_box = box_terrain(lambda h: h * h)

    def moments(c, _):
        start = pl.multiple_of(c * CHUNK * rows, CHUNK * rows)
        top = jnp.zeros((CHUNK, rows, LANES), F32)
        low = jnp.zeros((CHUNK, rows, LANES), F32)
        for t in range(tiles):
            cols = slice(t * LANES, (t + 1) * LANES)
            co = co_s[t, pl.ds(start, CHUNK * rows), :].reshape(CHUNK, rows, LANES)
            ph = ph_s[t, pl.ds(start, CHUNK * rows), :].reshape(CHUNK, rows, LANES)
            top += co * ph * terrain_box[None, :, cols]
            low += co * square_box[None, :, cols]
        mom[0, pl.ds(start, CHUNK * rows), :] = top.reshape(CHUNK * rows, LANES)
        mom[1, pl.ds(start, CHUNK * rows), :] = low.reshape(CHUNK * rows, LANES)
        return 0

    lax.fori_loop(0, chunks, moments, 0)

    def summed(index):
        total = mom[index, pl.ds(0, count, stride=rows), :]
        for j in range(1, rows):
            total += mom[index, pl.ds(j, count, stride=rows), :]
        if count < LANES:
            total = jnp.concatenate([total, jnp.zeros((LANES - count, LANES), F32)], axis=0)
        return jnp.sum(total.T, axis=0, keepdims=True)

    mom_all[my_row] = jnp.concatenate([summed(0), summed(1), jnp.zeros((6, LANES), F32)], axis=0)
    mom_copies = []
    for k in range(1, m):
        copy = remote(mom_all.at[my_row], mom_all.at[my_row], mom_sems, (k,), (me, lax.rem(my_row + k, m)))
        copy.start()
        mom_copies.append(copy)

    lax.fori_loop(0, chunks, take_edges, 0)
    edge_copies = start_pair(edge.at[0], edge.at[1], halo, halo_sems)
    for q in range(1, half - 1):
        smooth_rows(2 * q + 1, 2 * q + 3)
        w_copies.append(exchange(w_send, w_all, w_sems, q, 2 * q + 1, 2 * q + 3))

    date = lax.broadcasted_iota(jnp.int32, (KPAD, ifgs), 0)
    date = jnp.where(date >= DPAD, date - DPAD, date)
    signs = (date == pairs[1:2, :]).astype(F32) - (date == pairs[0:1, :]).astype(F32)
    gt[:, :ifgs] = signs[:DPAD].astype(BF16)
    gt[:, ifgs:] = signs[:DPAD].astype(BF16)
    g[...] = signs.T.astype(BF16)

    pixel = lax.broadcasted_iota(jnp.int32, (rows * LANES, 2 * LANES), 0)
    slot = lax.broadcasted_iota(jnp.int32, (rows * LANES, 2 * LANES), 1)
    first_pixel = jnp.where(slot < rows, slot * LANES, -1)
    last_pixel = jnp.where((slot >= LANES) & (slot < LANES + rows), (slot - LANES) * LANES + LANES - 1, -1)
    pick[...] = ((pixel == first_pixel) | (pixel == last_pixel)).astype(F32).astype(BF16)
    slot = lax.broadcasted_iota(jnp.int32, (2 * LANES, rows * LANES), 0)
    pixel = lax.broadcasted_iota(jnp.int32, (2 * LANES, rows * LANES), 1)
    first_pixel = jnp.where(slot < rows, slot * LANES, -1)
    last_pixel = jnp.where((slot >= LANES) & (slot < LANES + rows), (slot - LANES) * LANES + LANES - 1, -1)
    place[...] = ((pixel == first_pixel) | (pixel == last_pixel)).astype(F32).astype(BF16)

    for copy in mom_copies:
        copy.wait()
    sums = mom_all[0]
    for k in range(1, m):
        sums = sums + mom_all[k]
    slope = sums[0:1, :] / sums[1:2, :]
    topo_out[...] = slope[:, :count]
    topo_s[...] = jnp.broadcast_to(slope, (LANES, LANES)).T

    def correct_rows(low, high):
        def body(c, _):
            i0 = pl.multiple_of(c * CHUNK, CHUNK)
            column = topo_s[pl.ds(i0, CHUNK), :]
            for j in range(low, high):
                for d in range(n):
                    cols = pl.ds(d * LANES, LANES)
                    value = sm_s[j, pl.ds(i0, CHUNK), cols] - column * height[j:j + 1, cols]
                    c_send[d, j, pl.ds(i0, CHUNK), :] = value.astype(BF16)
            return 0

        lax.fori_loop(0, chunks, body, 0)

    c_copies = []
    for q in range(half - 1):
        correct_rows(2 * q + 1, 2 * q + 3)
        c_copies.append(exchange(c_send, c_all, c_sems, q, 2 * q + 1, 2 * q + 3))
    wait_pair(edge_copies, halo)
    last = []
    for part, j in ((half - 1, rows - 1), (half, 0)):
        smooth_rows(j, j + 1)
        last += exchange(w_send, w_all, w_sems, part, j, j + 1)
        correct_rows(j, j + 1)
        last += exchange(c_send, c_all, c_sems, part, j, j + 1)

    def pair(q):
        return 2 * q + 1, (2 * q + 2) % rows

    def both(q, of):
        return jnp.concatenate([of(j) for j in pair(q)], axis=1)

    def put(target, q, value):
        for i, j in enumerate(pair(q)):
            target[j] = value[:, i * LANES:(i + 1) * LANES]

    def back_project(u):
        return dot(gt[...], jnp.concatenate(split(u), axis=0))

    def right_rows(q):
        put(r_s, q, back_project(both(q, lambda j: w_all[j].astype(F32) * c_all[j].astype(F32))))

    def weighted(v, target, q):
        high, low = split(both(q, lambda j: v[j]))
        filler = jnp.zeros((KPAD - 2 * DPAD, 2 * LANES), BF16)
        diff = dot(g[...], jnp.concatenate([high, low, filler], axis=0))
        put(target, q, back_project(diff * both(q, lambda j: w_all[j].astype(F32))))

    small = lax.broadcasted_iota(jnp.int32, (DPAD, LANES), 1)

    def start_halo(v, step):
        left, right = (lax.max(me - 1, 0), my_row), (lax.min(me + 1, n - 1), my_row)
        copies = (
            (has_up, remote(pack.at[step, 0], halo_row.at[step, 1], row_sems, (step, 0), up)),
            (has_down, remote(pack.at[step, 1], halo_row.at[step, 0], row_sems, (step, 1), down)),
            (has_left, remote(pack.at[step, 2], halo_col.at[step, 1], col_sems, (step, 0), left)),
            (has_right, remote(pack.at[step, 3], halo_col.at[step, 0], col_sems, (step, 1), right)),
        )
        pack[step, 0] = v[0].astype(BF16)
        pack[step, 1] = v[rows - 1].astype(BF16)
        for there, copy in copies[:2]:
            pl.when(there)(copy.start)
        packed = dot(jnp.concatenate([v[j].astype(BF16) for j in range(rows)], axis=1), pick[...])
        pack[step, 2] = packed[:, :LANES].astype(BF16)
        pack[step, 3] = packed[:, LANES:].astype(BF16)
        for there, copy in copies[2:]:
            pl.when(there)(copy.start)
        return copies

    def wait_halo(copies, step):
        for there, copy in copies:
            pl.when(there)(copy.wait_send)
        for index, buffer in ((0, halo_row), (1, halo_col)):
            low_there, low_copy = copies[2 * index]
            high_there, high_copy = copies[2 * index + 1]
            for side, there, copy in ((0, low_there, high_copy), (1, high_there, low_copy)):
                pl.when(there)(copy.wait_recv)

                @pl.when(jnp.logical_not(there))
                def _(side=side, buffer=buffer):
                    buffer[step, side] = jnp.zeros((DPAD, LANES), BF16)

    def spread_and_halo(v, target, step, copies):
        for j in range(rows):
            here = v[j]
            around = jnp.where(small == 0, 0.0, pltpu.roll(here, 1, 1))
            around += jnp.where(small == LANES - 1, 0.0, pltpu.roll(here, LANES - 1, 1))
            if j:
                around += v[j - 1]
            if j < rows - 1:
                around += v[j + 1]
            spread = 4.0 * here - around
            target[j] = target[j] + SMOOTHING_WEIGHT * spread + RIDGE_WEIGHT * here
        wait_halo(copies, step)
        beside = dot(jnp.concatenate([halo_col[step, 0], halo_col[step, 1]], axis=1), place[...])
        for j in range(rows):
            around = beside[:, j * LANES:(j + 1) * LANES]
            if j == 0:
                around = around + halo_row[step, 0].astype(F32)
            if j == rows - 1:
                around = around + halo_row[step, 1].astype(F32)
            target[j] = target[j] - SMOOTHING_WEIGHT * around

    def apply(v, target, step, middle):
        copies = start_halo(v, step)
        for q in range(half):
            weighted(v, target, q)
            if q == half // 2 - 1:
                middle()
        spread_and_halo(v, target, step, copies)

    def fold(value):
        return jnp.sum(value, axis=0, keepdims=True)

    def reduce_first(step, parts):
        filled = list(parts) + [jnp.zeros((8 - len(parts), LANES), F32)]
        red_b[step, my_row] = jnp.concatenate(filled, axis=0)
        copies = []
        for k in range(1, m):
            copy = remote(red_b.at[step, my_row], red_b.at[step, my_row], b_sems, (step, k), (me, lax.rem(my_row + k, m)))
            copy.start()
            copies.append(copy)
        return copies

    def reduce_second(step, copies):
        for copy in copies:
            copy.wait()
        total = red_b[step, 0]
        for k in range(1, m):
            total = total + red_b[step, k]
        red_a[step, me] = total
        later = []
        for k in range(1, n):
            copy = remote(red_a.at[step, me], red_a.at[step, me], a_sems, (step, k), (lax.rem(me + k, n), my_row))
            copy.start()
            later.append(copy)
        return later

    def reduce_last(step, copies):
        for copy in copies:
            copy.wait()
        total = red_a[step, 0]
        for k in range(1, n):
            total = total + red_a[step, k]
        total = jnp.sum(total, axis=1, keepdims=True)
        return [total[i:i + 1, :] for i in range(3)]

    def overlapped(step, parts, v, target, apply_step):
        state = {"copies": reduce_first(step, parts)}

        def middle():
            state["copies"] = reduce_second(step, state["copies"])

        apply(v, target, apply_step, middle)
        return reduce_last(step, state["copies"])

    for q in range(half - 1):
        for copy in w_copies[q] + c_copies[q]:
            copy.wait()
        right_rows(q)
        weighted(r_s, w_s, q)
    for copy in last:
        copy.wait()
    right_rows(half - 1)
    copies = start_halo(r_s, 0)
    weighted(r_s, w_s, half - 1)
    spread_and_halo(r_s, w_s, 0, copies)
    gamma_sum = jnp.zeros((1, LANES), F32)
    delta_sum = jnp.zeros((1, LANES), F32)
    for j in range(rows):
        gamma_sum += fold(r_s[j] * r_s[j])
        delta_sum += fold(r_s[j] * w_s[j])
    gamma, curve, _ = overlapped(0, (gamma_sum, delta_sum), w_s, n_s, 1)

    alpha = gamma / curve
    alpha_first = alpha
    gamma_sum = jnp.zeros((1, LANES), F32)
    delta_sum = jnp.zeros((1, LANES), F32)
    cross_sum = jnp.zeros((1, LANES), F32)
    for j in range(rows):
        p, s, z = r_s[j], w_s[j], n_s[j]
        r = p - alpha * s
        w = s - alpha * z
        p_s[j], s_s[j], z_s[j] = p, s, z
        r_s[j], w_s[j] = r, w
        gamma_sum += fold(r * r)
        delta_sum += fold(r * w)
        cross_sum += fold(r * s)
    gamma_next, delta, cross = overlapped(1, (gamma_sum, delta_sum, cross_sum), w_s, n_s, 2)

    beta = gamma_next / gamma
    gamma = gamma_next
    curve = delta + 2.0 * beta * cross + beta * beta * curve
    alpha = gamma / curve
    gamma_sum = jnp.zeros((1, LANES), F32)
    delta_sum = jnp.zeros((1, LANES), F32)
    cross_sum = jnp.zeros((1, LANES), F32)
    for j in range(rows):
        r, w = r_s[j], w_s[j]
        first_p = p_s[j]
        p = r + beta * first_p
        s = w + beta * s_s[j]
        z = n_s[j] + beta * z_s[j]
        r = r - alpha * s
        w = w - alpha * z
        p_s[j] = p
        r_s[j] = r
        z_s[j] = alpha_first * first_p + alpha * p
        gamma_sum += fold(r * r)
        delta_sum += fold(r * w)
        cross_sum += fold(r * s)
    copies = reduce_first(2, (gamma_sum, delta_sum, cross_sum))
    gamma_next, delta, cross = reduce_last(2, reduce_second(2, copies))
    beta = gamma_next / gamma
    curve = delta + 2.0 * beta * cross + beta * beta * curve
    alpha = gamma_next / curve
    for j in range(rows):
        x_out[j] = z_s[j] + alpha * (r_s[j] + beta * p_s[j])


def order_dates(x, topo, out, topo_out):
    rows, dates, _ = x.shape
    for j in range(rows):
        out[pl.ds(j, dates, stride=rows), :] = x[j]
    topo_out[...] = topo[...]


def solution(mesh):
    n, m = mesh.shape["ifg"], mesh.shape["rows"]

    def per_device(phase, coherence, height, gap_mask, date_pairs):
        count, rows, width = phase.shape
        ifgs = date_pairs.shape[0]
        tiles = width // LANES
        dma = pltpu.SemaphoreType.DMA
        state = pltpu.VMEM((rows, DPAD, LANES), F32)
        vmem = pl.BlockSpec(memory_space=pltpu.VMEM)
        field, topo = pl.pallas_call(
            functools.partial(kernel, n, m),
            out_shape=(
                jax.ShapeDtypeStruct((rows, DPAD, LANES), F32),
                jax.ShapeDtypeStruct((1, count), F32),
            ),
            in_specs=[vmem] * 5,
            out_specs=(vmem, vmem),
            scratch_shapes=[
                pltpu.VMEM((tiles, count * rows, LANES), F32),
                pltpu.VMEM((tiles, count * rows, LANES), F32),
                pltpu.VMEM((2, 2, count, width), BF16),
                pltpu.VMEM((2, 2, count, width), BF16),
                pltpu.VMEM((rows, count, width), F32),
                pltpu.VMEM((n, rows, count, LANES), BF16),
                pltpu.VMEM((rows, ifgs, LANES), BF16),
                pltpu.VMEM((n, rows, count, LANES), BF16),
                pltpu.VMEM((rows, ifgs, LANES), BF16),
                pltpu.VMEM((2, rows, width), F32),
                pltpu.VMEM((count, rows), F32),
                pltpu.VMEM((2, count * rows, LANES), F32),
                pltpu.VMEM((m, 8, LANES), F32),
                pltpu.VMEM((LANES, LANES), F32),
                pltpu.VMEM((ifgs, KPAD), BF16),
                pltpu.VMEM((DPAD, 2 * ifgs), BF16),
                pltpu.VMEM((rows * LANES, 2 * LANES), BF16),
                pltpu.VMEM((2 * LANES, rows * LANES), BF16),
                state, state, state, state, state, state,
                pltpu.VMEM((3, 4, DPAD, LANES), BF16),
                pltpu.VMEM((3, 2, DPAD, LANES), BF16),
                pltpu.VMEM((3, 2, DPAD, LANES), BF16),
                pltpu.VMEM((3, n, 8, LANES), F32),
                pltpu.VMEM((3, m, 8, LANES), F32),
                dma((2, 2)),
                dma((2, 2)),
                dma((2, rows // 2 + 1, n)),
                dma((2, rows // 2 + 1, n)),
                dma((2, m)),
                dma((2, 3, 2)),
                dma((2, 3, 2)),
                dma((2, 3, n)),
                dma((2, 3, m)),
            ],
            compiler_params=pltpu.CompilerParams(
                collective_id=0, has_side_effects=True, vmem_limit_bytes=56 * 1024 * 1024
            ),
        )(phase, coherence, height, gap_mask.T, date_pairs.T)
        displacement, topo = pl.pallas_call(
            order_dates,
            grid=(pl.cdiv(DATES, BLOCK),),
            out_shape=(
                jax.ShapeDtypeStruct((DATES * rows, LANES), F32),
                jax.ShapeDtypeStruct((1, count), F32),
            ),
            in_specs=[
                pl.BlockSpec((rows, BLOCK, LANES), lambda i: (0, i, 0)),
                pl.BlockSpec((1, count), lambda i: (0, 0)),
            ],
            out_specs=(
                pl.BlockSpec((BLOCK * rows, LANES), lambda i: (i, 0)),
                pl.BlockSpec((1, count), lambda i: (0, 0)),
            ),
        )(field, topo)
        return displacement.reshape(DATES, rows, LANES), topo.reshape(count)

    return jax.shard_map(
        per_device,
        mesh=mesh,
        in_specs=(
            P("ifg", "rows", None),
            P("ifg", "rows", None),
            P("rows", None),
            P("ifg", "rows"),
            P(),
        ),
        out_specs=(P(None, "rows", "ifg"), P("ifg")),
        check_vma=False,
    )
```
